512 devices in a mesh: grp: 16 (over z, core), row: 32 (over y, x).
Axes of the slice: x: 4, y: 8, z: 8, core: 2. Of those that a mesh axis runs over, the one named last changes fastest.
Arguments:
- leaf_rhs: float32 [32, 16, 256, 128], P('row', 'grp'), may hold values from -6 to 6
- leaf_inv: float32 [32, 16, 256, 256], P('row', 'grp'), may hold values from -0.15625 to 1.15625, as said below
- leaf_panel: float32 [32, 16, 6, 256, 256], P('row', 'grp'), may hold values from -0.15625 to 0.15625
- leaf_mask: int32 [32, 16, 6], P('row', 'grp'), may hold values 0 or 1
- inner_rhs: float32 [32, 256, 128], P('row', 'grp'), may hold values from -6 to 6
- inner_inv: float32 [32, 256, 256], P('row', 'grp'), may hold values from -0.15625 to 1.15625, as said below
- inner_panel: float32 [32, 6, 256, 256], P('row', None, 'grp'), may hold values from -0.15625 to 0.15625, as said below
Outputs:
- leaf_solution: float32 [32, 16, 256, 128], P('row', 'grp')
- inner_solution: float32 [32, 256, 128], P('row', 'grp')
The draws below stay inside these ranges and needn't reach their ends.
Inputs may be any that keep to these rules, and one draw needn't show every extreme that they name: `leaf_inv`: identity plus a full matrix of independent entries; diagonal entries near 1, off-diagonal entries small. `inner_inv`: identity plus a full matrix of independent entries; diagonal entries near 1, off-diagonal entries small. `inner_panel`: blocks for levels at or below the supernode's own level are not used.
All inputs are finite; a program needn't handle non-finite values. No bound on the sum of `leaf_mask` on one device may be relied on, other than what follows from the above.
Results may differ from the reference program's by a relative error of at most 0.0003.
Values sent between devices are 32-bit elements; how exact they have to be, the bound alone decides.
A program may use at most 64 MiB of HBM per device.

```python
import jax
import jax.numpy as jnp
import numpy as np
from jax import lax

WIDTH = 256
RHS = 128
LEAVES = 16
LEVELS = 6
N_ROW = 32


def inverse_block(raw):
    rows = jnp.arange(WIDTH)
    eye = (rows[:, None] == rows[None, :]).astype(jnp.float32)
    return eye + 0.5 * raw / WIDTH ** 0.5


def level_scale(nleaves):
    steps = jnp.arange(LEVELS)
    span = jnp.minimum(2.0 ** (steps + 1), N_ROW * 1.0)
    return 0.5 / WIDTH ** 0.5 / (nleaves * span) ** 0.25


def draw_leaf_inv(key, part):
    key = jax.random.fold_in(key, 11)
    shape = (N_ROW, LEAVES, WIDTH, WIDTH)
    raw = jax.random.truncated_normal(key, -4.0, 4.0, shape, jnp.float32)
    return inverse_block(raw)


def draw_inner_inv(key, part):
    key = jax.random.fold_in(key, 12)
    shape = (N_ROW, WIDTH, WIDTH)
    raw = jax.random.truncated_normal(key, -4.0, 4.0, shape, jnp.float32)
    return inverse_block(raw)


def draw_leaf_panel(key, part):
    key = jax.random.fold_in(key, 13)
    shape = (N_ROW, LEAVES, LEVELS, WIDTH, WIDTH)
    raw = jax.random.truncated_normal(key, -4.0, 4.0, shape, jnp.float32)
    return raw * level_scale(LEAVES * 1.0)[None, None, :, None, None]


def draw_inner_panel(key, part):
    key = jax.random.fold_in(key, 14)
    shape = (N_ROW, LEVELS, WIDTH, WIDTH)
    raw = jax.random.truncated_normal(key, -4.0, 4.0, shape, jnp.float32)
    return raw * level_scale(LEAVES * 1.0)[None, :, None, None]


def set_ends(array, stream_key, smallest, top_value):
    longest = array.shape.index(max(array.shape))
    spots = []
    for shift in (0, 1):
        where = [jax.random.randint(jax.random.fold_in(stream_key, axis), (), 0, length) for axis, length in enumerate(array.shape)]
        where[longest] = (where[longest] + shift) % array.shape[longest]
        spots.append(tuple(where))
    return array.at[spots[0]].set(smallest).at[spots[1]].set(top_value)


def level_of(own_key, dims, pieces, smallest, top_value):
    gain, own = 1.0, jax.random.fold_in(own_key, 6)
    for dim, parts in pieces:
        heights = jnp.exp(jax.random.uniform(jax.random.fold_in(own, dim), (parts,), jnp.float32, smallest / len(pieces), top_value / len(pieces)))
        gain = gain * jnp.repeat(heights, dims[dim] // parts).reshape([-1 if axis == dim else 1 for axis in range(len(dims))])
    return gain


def scatter_about(stream_key, shape, width, reach, pieces=(), held_as=jnp.bfloat16):
    loudness = level_of(stream_key, shape, pieces, -0.22, 0.18) if pieces else 1.0
    entries = jax.random.normal(stream_key, shape, jnp.float32) * width * loudness
    return jnp.minimum(jnp.maximum(entries, -reach), reach).astype(held_as)


def setup_inputs(seed: int = 0) -> dict:
    keys = jax.random.split(jax.random.key(seed), 8)
    leaf_rhs = scatter_about(keys[0], (N_ROW, LEAVES, WIDTH, RHS), 1.0, 6.0, ((0, 32), (1, 16)), jnp.float32)
    leaf_inv = draw_leaf_inv(jax.random.fold_in(keys[7], 71), 0)
    leaf_panel = draw_leaf_panel(jax.random.fold_in(keys[7], 71), 0)
    leaf_mask = set_ends((jax.random.randint(keys[3], (N_ROW, LEAVES, LEVELS), 0, 4) < 3).astype(jnp.int32), jax.random.fold_in(keys[3], 1), 0, 1)
    inner_rhs = scatter_about(keys[4], (N_ROW, WIDTH, RHS), 1.0, 6.0, ((0, 32), (1, 16)), jnp.float32)
    inner_inv = draw_inner_inv(jax.random.fold_in(keys[7], 71), 0)
    inner_panel = draw_inner_panel(jax.random.fold_in(keys[7], 71), 0)
    return {"leaf_rhs": leaf_rhs, "leaf_inv": leaf_inv, "leaf_panel": leaf_panel, "leaf_mask": leaf_mask, "inner_rhs": inner_rhs, "inner_inv": inner_inv, "inner_panel": inner_panel}


def tree_levels(count, levels):
    table = np.zeros(count, np.int64)
    for place in range(count):
        if place == 0:
            table[place] = levels
        else:
            zeros_low = 0
            while place % (2 ** (zeros_low + 1)) == 0:
                zeros_low += 1
            table[place] = zeros_low + 1
    return table


def reference(leaf_rhs, leaf_inv, leaf_panel, leaf_mask, inner_rhs, inner_inv, inner_panel):
    highest = lax.Precision.HIGHEST
    count = N_ROW
    levels = LEVELS
    own_level = tree_levels(count, levels)
    masked = leaf_panel * leaf_mask.astype(jnp.float32)[:, :, :, None, None]
    leaf_fwd = jnp.einsum("jlnk,jlkr->jlnr", leaf_inv, leaf_rhs, precision=highest)
    leaf_terms = jnp.einsum("jlkna,jlnr->jkar", masked, leaf_fwd, precision=highest)
    inner_fwd = jnp.zeros((count, WIDTH, RHS), jnp.float32)
    for step in range(levels):
        level = step + 1
        span = min(2 ** level, count)
        below = jnp.asarray((own_level < level).astype(np.float32), dtype=jnp.float32)
        inner_term = jnp.einsum("jna,jnr->jar", inner_panel[:, step], inner_fwd, precision=highest)
        contrib = leaf_terms[:, step] + below[:, None, None] * inner_term
        grouped = contrib.reshape(count // span, span, WIDTH, RHS).sum(axis=1)
        owners = np.arange(count // span) * span + (span // 2 if level < levels else 0)
        pending = inner_rhs[owners] - grouped
        solved = jnp.einsum("gnk,gkr->gnr", inner_inv[owners], pending, precision=highest)
        inner_fwd = inner_fwd.at[owners].set(solved)
    inner_back = jnp.zeros((count, WIDTH, RHS), jnp.float32)
    inner_acc = jnp.zeros((count, WIDTH, RHS), jnp.float32)
    leaf_acc = jnp.zeros(leaf_rhs.shape, jnp.float32)
    for step in reversed(range(levels)):
        level = step + 1
        span = min(2 ** level, count)
        below = jnp.asarray((own_level < level).astype(np.float32), dtype=jnp.float32)
        owners = np.arange(count // span) * span + (span // 2 if level < levels else 0)
        rest = inner_fwd[owners] - inner_acc[owners]
        solved = jnp.einsum("gkn,gkr->gnr", inner_inv[owners], rest, precision=highest)
        inner_back = inner_back.at[owners].set(solved)
        spread = jnp.repeat(solved, span, axis=0)
        leaf_acc = leaf_acc + jnp.einsum("jlna,jar->jlnr", masked[:, :, step], spread, precision=highest)
        inner_acc = inner_acc + below[:, None, None] * jnp.einsum("jna,jar->jnr", inner_panel[:, step], spread, precision=highest)
    leaf_back = jnp.einsum("jlkn,jlkr->jlnr", leaf_inv, leaf_fwd - leaf_acc, precision=highest)
    return leaf_back, inner_back
```

```python
import functools

import jax
import jax.numpy as jnp
from jax import lax
from jax.experimental import pallas as pl
from jax.experimental.pallas import tpu as pltpu
from jax.sharding import PartitionSpec as P

F32 = jnp.float32
BF16 = jnp.bfloat16
NN = (((1,), (0,)), ((), ()))
NT = (((1,), (1,)), ((), ()))


def split(x):
    high = x.astype(BF16)
    return high, (x - high.astype(F32)).astype(BF16)


def dot(a, b, dims):
    return lax.dot_general(a, b, dims, preferred_element_type=F32)


def product(a, b, dims=NN):
    return dot(a[0], b[0], dims) + (dot(a[0], b[1], dims) + dot(a[1], b[0], dims))


def thin(x, w, dims):
    rows = x.shape[0]
    high = x.astype(BF16).astype(F32)
    both = jnp.concatenate([high, x - high], axis=0).astype(BF16)
    first, second = dot(both, w[0], dims), dot(both, w[1], dims)
    return first[:rows] + (first[rows:] + second[:rows])


def kernel(
    chips, count,
    rhs_h, inv_h, pan_h, mask_s, irhs_h, iinv_h, ipan_h,
    leaf_out, inner_out,
    v_rhs, v_inv, v_pan, i_hi, i_lo, p_hi, p_lo, leaf_t,
    terms, terms_in, pieces, upd,
    blocks, rblock, rhs_t, b_hi, b_lo,
    child_in, lat_in, pend, fwd, acc, sol, full, leaf_acc, turned,
    in_sem, own_sem, ring_recv, ring_send, sib_recv, sib_send,
    t_recv, t_send, a_recv, a_send, lat_recv, lat_send,
    up_recv, up_send, down_recv, down_send,
    ag_recv, ag_send, pair_recv, pair_send,
):
    top = pan_h.shape[0]
    width, nrhs = v_rhs.shape
    member = lax.axis_index("grp")
    j = lax.axis_index("row")
    z, c = lax.div(member, 2), lax.rem(member, 2)
    other = 1 - c
    lev, low = jnp.int32(1), jnp.int32(1)
    for bit in range(1, top):
        even = (lax.rem(j, 2**bit) == 0).astype(jnp.int32)
        lev, low = lev + even, low * (1 + even)
    is_top = lev == top
    has_child = lev >= 2
    two_children = jnp.logical_and(has_child, lev < top)
    parent = lax.div(j, low * 4) * low * 4 + low * 2
    parent = jnp.where(lev == top - 1, 0, parent)
    slot = lax.rem(lax.div(j, low * 2), 2)
    child0 = lax.rem(j - lax.div(low, 2) + count, count)
    child1 = lax.rem(j + lax.div(low, 2), count)
    above = lax.rem(j - low + count, count)

    def at(zz=None, cc=None, jj=None):
        zz = z if zz is None else zz
        cc = c if cc is None else cc
        return {"grp": zz * 2 + cc, "row": j if jj is None else jj}

    def turn(step):
        return lax.rem(z + step + chips, chips)

    def remote(src, dst, send, recv, where):
        return pltpu.make_async_remote_copy(
            src_ref=src, dst_ref=dst, send_sem=send, recv_sem=recv,
            device_id=where, device_id_type=pl.DeviceIdType.MESH,
        )

    def await_bytes(ref, sem):
        pltpu.make_async_copy(ref, ref, sem).wait()

    def local(src, dst, sem):
        return pltpu.make_async_copy(src, dst, sem)

    def own_copies(b):
        return local(ipan_h.at[b], blocks.at[b, z, c], own_sem.at[b])

    local(rhs_h, v_rhs, in_sem.at[top]).start()
    local(inv_h, v_inv, in_sem.at[top + 1]).start()
    own_inv = local(iinv_h, blocks.at[0, z, c], own_sem.at[0])
    own_rhs = local(irhs_h, rblock.at[z, c], own_sem.at[top])
    own_inv.start()
    own_rhs.start()

    @pl.loop(lev, top)
    def _(b):
        own_copies(b).start()

    for step in range(top):
        local(pan_h.at[step], v_pan.at[step], in_sem.at[step]).start()

    barrier = pltpu.get_barrier_semaphore()

    def greet(where):
        pl.semaphore_signal(barrier, inc=1, device_id=where, device_id_type=pl.DeviceIdType.MESH)

    greet(at(cc=other))
    for step in range(1, chips):
        greet(at(zz=turn(step)))

    @pl.when(lev < top)
    def _():
        greet(at(jj=parent))
        greet(at(jj=above))

    @pl.when(has_child)
    def _():
        greet(at(jj=child0))

    @pl.when(two_children)
    def _():
        greet(at(jj=child1))

    for level in range(1, top):
        @pl.when(lev > level)
        def _(level=level):
            greet(at(jj=lax.rem(j + 2 ** (level - 1), count)))

    expected = chips + (lev - 1) + has_child.astype(jnp.int32)
    expected = expected + two_children.astype(jnp.int32) + 2 * (lev < top).astype(jnp.int32)
    pl.semaphore_wait(barrier, expected)

    right, left = chips // 2, chips - 1 - chips // 2

    def shard(b, zz):
        return rblock.at[zz, c] if b is None else blocks.at[b, zz, c]

    def sem_of(b):
        return top if b is None else b

    def ring(b, way, step):
        src = turn(-step if way == 0 else step)
        ref = shard(b, src)
        target = turn(1 if way == 0 else -1)
        i = sem_of(b)
        return remote(ref, ref, ring_send.at[i], ring_recv.at[way, step, i], at(zz=target))

    def ring_arrived(b, way, step):
        src = turn(-step - 1 if way == 0 else step + 1)
        await_bytes(shard(b, src), ring_recv.at[way, step, sem_of(b)])

    def each_block(body):
        body(0)
        body(None)
        pl.loop(lev, top)(body)

    def first_step(b):
        if b is None:
            own_rhs.wait()
        elif isinstance(b, int):
            own_inv.wait()
        else:
            own_copies(b).wait()
        if right:
            ring(b, 0, 0).start()
        if left:
            ring(b, 1, 0).start()

    each_block(first_step)

    def next_step(step):
        def body(b):
            if step <= right:
                ring_arrived(b, 0, step - 1)
                if step < right:
                    ring(b, 0, step).start()
            if step <= left:
                ring_arrived(b, 1, step - 1)
                if step < left:
                    ring(b, 1, step).start()
        each_block(body)

    local(rhs_h, v_rhs, in_sem.at[top]).wait()
    local(inv_h, v_inv, in_sem.at[top + 1]).wait()
    hi, lo = split(v_inv[...])
    i_hi[...] = hi
    i_lo[...] = lo
    forward = product((hi, lo), split(v_rhs[...])).T
    leaf_t[...] = forward
    forward = split(forward)

    @pl.loop(0, top)
    def _(step):
        local(pan_h.at[step], v_pan.at[step], in_sem.at[step]).wait()
        hi, lo = split(v_pan[step])
        p_hi[step] = hi
        p_lo[step] = lo
        term = product(forward, (hi, lo)) * mask_s[step].astype(F32)
        terms[:, :, step] = term.reshape(2, chips, -1, width)
        remote(
            terms.at[other, :, step], terms_in.at[:, step],
            t_send, t_recv.at[step], at(cc=other),
        ).start()

    groups = [(0, 1), (1, top)]
    for number, (first, last) in enumerate(groups):
        @pl.loop(first, last)
        def _(step):
            await_bytes(terms_in.at[:, step], t_recv.at[step])
            terms[c, :, step] = terms[c, :, step] + terms_in[:, step]

        for step in range(1, chips):
            zz = turn(step)
            remote(
                terms.at[c, zz, first:last], pieces.at[z, first:last],
                a_send, a_recv.at[number], at(zz=zz),
            ).start()

    for step in range(1, max(right, left) + 1):
        next_step(step)

    def share_block(b):
        ref = rblock.at[:, c] if b is None else blocks.at[b, :, c]
        i = sem_of(b)
        remote(ref, ref, sib_send.at[i], sib_recv.at[i], at(cc=other)).start()

    each_block(share_block)

    for number, (first, last) in enumerate(groups):
        if chips > 1:
            await_bytes(pieces.at[0 : chips - 1, first:last], a_recv.at[number])
        total = terms[c, z, first:last]
        for step in range(1, chips):
            total = total + pieces[turn(step), first:last]
        upd[first:last] = total

    def lateral_up(level):
        l = level - 1
        return remote(
            upd.at[l], lat_in, lat_send.at[l], lat_recv,
            at(jj=lax.rem(j + 2**l, count)),
        )

    for level in range(1, top):
        @pl.when(lev > level)
        def _(level=level):
            lateral_up(level).start()

    def take_block(b):
        if b is None:
            await_bytes(rblock.at[:, other], sib_recv.at[top])
            rhs_t[...] = rblock[...].reshape(width, nrhs).T.reshape(rhs_t.shape)
        else:
            await_bytes(blocks.at[b, :, other], sib_recv.at[b])
            hi, lo = split(blocks[b].reshape(width, width))
            b_hi[b] = hi
            b_lo[b] = lo

    each_block(take_block)

    own = lev - 1
    pend[...] = rhs_t[c, z] - upd[own]

    @pl.when(has_child)
    def _():
        await_bytes(child_in.at[0, own], up_recv.at[0, own])
        pend[...] = pend[...] - child_in[0, own]

    @pl.when(two_children)
    def _():
        await_bytes(child_in.at[1, own], up_recv.at[1, own])
        pend[...] = pend[...] - child_in[1, own]

    @pl.when(lev < top)
    def _():
        await_bytes(lat_in, lat_recv)
        pend[...] = pend[...] - lat_in[...]

    fwd[...] = thin(pend[...], (b_hi[0], b_lo[0]), NT)

    def send_up(l):
        return remote(
            upd.at[l], child_in.at[slot, l], up_send.at[l], up_recv.at[slot, l], at(jj=parent)
        )

    @pl.loop(lev, top)
    def _(l):
        upd[l] = upd[l] + thin(fwd[...], (b_hi[l], b_lo[l]), NN)

        @pl.when(has_child)
        def _():
            await_bytes(child_in.at[0, l], up_recv.at[0, l])
            await_bytes(child_in.at[1, l], up_recv.at[1, l])
            upd[l] = upd[l] + child_in[0, l] + child_in[1, l]

        send_up(l).start()

    acc[...] = jnp.zeros_like(acc)
    leaf_acc[...] = jnp.zeros_like(leaf_acc)

    def send_down(l, which):
        target = (child0, child1, above)[which]
        return remote(
            sol.at[l], sol.at[l], down_send.at[which, l], down_recv.at[l], at(jj=target)
        )

    def spread(l, step):
        zz = turn(step)
        return remote(sol.at[l], full.at[l, c, z], ag_send.at[l], ag_recv.at[l], at(zz=zz))

    def pair(l):
        return remote(full.at[l, c], full.at[l, c], pair_send.at[l], pair_recv.at[l], at(cc=other))

    def descend(l):
        @pl.when(l + 1 > lev)
        def _():
            await_bytes(sol.at[l], down_recv.at[l])

            @pl.when(has_child)
            def _():
                send_down(l, 0).start()
                send_down(l, 1).start()

            acc[...] = acc[...] + thin(sol[l], (b_hi[l], b_lo[l]), NT)

        @pl.when(l + 1 == lev)
        def _():
            sol[l] = thin(fwd[...] - acc[...], (b_hi[0], b_lo[0]), NN)

            @pl.when(has_child)
            def _():
                send_down(l, 0).start()

            @pl.when(two_children)
            def _():
                send_down(l, 1).start()

            @pl.when(lev < top)
            def _():
                send_down(l, 2).start()

        @pl.when(l + 1 < lev)
        def _():
            await_bytes(sol.at[l], down_recv.at[l])

        for step in range(1, chips):
            spread(l, step).start()
        full[l, c, z] = sol[l]

    def join(l):
        if chips > 1:
            await_bytes(full.at[l, c, 0 : chips - 1], ag_recv.at[l])
        pair(l).start()

    def leaf_back(l):
        await_bytes(full.at[l, other], pair_recv.at[l])
        ancestor = split(full[l].reshape(nrhs, width))
        leaf_acc[...] = leaf_acc[...] + mask_s[l].astype(F32) * product(
            ancestor, (p_hi[l], p_lo[l]), NT
        )

    @pl.loop(0, top + 2)
    def _(i):
        l = top - 1 - i

        @pl.when(i < top)
        def _():
            descend(l)

        @pl.when(jnp.logical_and(i >= 1, i < top + 1))
        def _():
            join(l + 1)

        @pl.when(i >= 2)
        def _():
            leaf_back(l + 2)

    rest = split(leaf_t[...] - leaf_acc[...])
    leaf_out[...] = product(rest, (i_hi[...], i_lo[...])).T
    share = inner_out.shape[0]
    turned[...] = full[own].reshape(nrhs, width).T
    inner_out[...] = turned[pl.ds(pl.multiple_of(member * share, share), share), :]

    def sent_block(b):
        i = sem_of(b)
        if chips > 1:
            ref = rblock.at[0 : chips - 1, 0] if b is None else blocks.at[b, 0 : chips - 1, 0]
            await_bytes(ref, ring_send.at[i])
        ref = rblock.at[:, c] if b is None else blocks.at[b, :, c]
        await_bytes(ref, sib_send.at[i])

    each_block(sent_block)
    await_bytes(terms.at[0], t_send)
    if chips > 1:
        await_bytes(terms.at[0, 0 : chips - 1], a_send)
    for level in range(1, top):
        @pl.when(lev > level)
        def _(level=level):
            lateral_up(level).wait_send()

    @pl.loop(lev, top)
    def _(l):
        send_up(l).wait_send()

    @pl.loop(own, top)
    def _(l):
        @pl.when(has_child)
        def _():
            send_down(l, 0).wait_send()

        @pl.when(two_children)
        def _():
            send_down(l, 1).wait_send()

    @pl.when(lev < top)
    def _():
        send_down(own, 2).wait_send()

    @pl.loop(0, top)
    def _(l):
        if chips > 1:
            await_bytes(full.at[l, 0, 0 : chips - 1], ag_send.at[l])
        pair(l).wait_send()


def per_device(leaf_rhs, leaf_inv, leaf_panel, leaf_mask, inner_rhs, inner_inv, inner_panel):
    members, count = lax.axis_size("grp"), lax.axis_size("row")
    chips = members // 2
    width, nrhs = leaf_rhs.shape[2:]
    top = leaf_panel.shape[2]
    share, cols = width // members, nrhs // members
    hbm = pl.BlockSpec(memory_space=pl.ANY)
    dma = pltpu.SemaphoreType.DMA
    steps = max(chips // 2, 1)
    v = pltpu.VMEM
    call = pl.pallas_call(
        functools.partial(kernel, chips, count),
        out_shape=(
            jax.ShapeDtypeStruct((width, nrhs), F32),
            jax.ShapeDtypeStruct((share, nrhs), F32),
        ),
        in_specs=[hbm, hbm, hbm, pl.BlockSpec(memory_space=pltpu.SMEM), hbm, hbm, hbm],
        out_specs=[pl.BlockSpec(memory_space=pltpu.VMEM)] * 2,
        scratch_shapes=[
            v((width, nrhs), F32),
            v((width, width), F32),
            v((top, width, width), F32),
            v((width, width), BF16),
            v((width, width), BF16),
            v((top, width, width), BF16),
            v((top, width, width), BF16),
            v((nrhs, width), F32),
            v((2, chips, top, cols, width), F32),
            v((chips, top, cols, width), F32),
            v((chips, top, cols, width), F32),
            v((top, cols, width), F32),
            v((top, chips, 2, share, width), F32),
            v((chips, 2, share, nrhs), F32),
            v((2, chips, cols, width), F32),
            v((top, width, width), BF16),
            v((top, width, width), BF16),
            v((2, top, cols, width), F32),
            v((cols, width), F32),
            v((cols, width), F32),
            v((cols, width), F32),
            v((cols, width), F32),
            v((top, cols, width), F32),
            v((top, 2, chips, cols, width), F32),
            v((nrhs, width), F32),
            v((width, nrhs), F32),
            dma((top + 2,)),
            dma((top + 1,)),
            dma((2, steps, top + 1)),
            dma((top + 1,)),
            dma((top + 1,)),
            dma((top + 1,)),
            dma((top,)),
            dma,
            dma((2,)),
            dma,
            dma,
            dma((top,)),
            dma((2, top)),
            dma((top,)),
            dma((top,)),
            dma((3, top)),
            dma((top,)),
            dma((top,)),
            dma((top,)),
            dma((top,)),
        ],
        compiler_params=pltpu.CompilerParams(
            collective_id=0, has_side_effects=True, vmem_limit_bytes=48 * 2**20
        ),
    )
    leaf, inner = call(
        leaf_rhs[0, 0], leaf_inv[0, 0], leaf_panel[0, 0], leaf_mask[0, 0],
        inner_rhs[0], inner_inv[0], inner_panel[0],
    )
    return leaf[None, None], inner[None]


def solution(mesh):
    in_specs = (
        P("row", "grp", None, None),
        P("row", "grp", None, None),
        P("row", "grp", None, None, None),
        P("row", "grp", None),
        P("row", "grp", None),
        P("row", "grp", None),
        P("row", None, "grp", None),
    )
    out_specs = (P("row", "grp", None, None), P("row", "grp", None))
    return jax.shard_map(
        per_device, mesh=mesh, in_specs=in_specs, out_specs=out_specs, check_vma=False
    )
```

```python
import functools

import jax
import jax.numpy as jnp
from jax import lax
from jax.experimental import pallas as pl
from jax.experimental.pallas import tpu as pltpu
from jax.sharding import PartitionSpec as P

F32 = jnp.float32
BF16 = jnp.bfloat16
NN = (((1,), (0,)), ((), ()))
NT = (((1,), (1,)), ((), ()))
EIGHT = 8


def split(x):
    high = x.astype(BF16)
    return high, (x - high.astype(F32)).astype(BF16)


def dot(a, b, dims):
    return lax.dot_general(a, b, dims, preferred_element_type=F32)


def product(a, b, dims=NN):
    return dot(a[0], b[0], dims) + (dot(a[0], b[1], dims) + dot(a[1], b[0], dims))


def thin(x, w, dims):
    rows = x.shape[0]
    high = x.astype(BF16).astype(F32)
    both = jnp.concatenate([high, x - high], axis=0).astype(BF16)
    first, second = dot(both, w[0], dims), dot(both, w[1], dims)
    return first[:rows] + (first[rows:] + second[:rows])


class Plan:
    def __init__(self, top, count):
        self.groups = count // EIGHT
        self.host3 = 14 if count > EIGHT else 6
        order = [(2, 0)] + [(2, l) for l in range(3, top + 1)] + [(6, 0), (6, 3), (4, 0)]
        for l in range(4, top + 1):
            order += [(6, l), (4, l)]
        self.mid = {key: i for i, key in enumerate(order)}
        self.mid_local = top - 1
        self.mid_rhs = {2: 0, 6: 1, 4: 2}
        self.nodes = []
        for l in range(4, top):
            self.nodes += [(l, a) for a in range(2 ** (l - 1), count, 2**l)]
        self.nodes.append((top, 0))
        self.covers = {}
        for l, a in self.nodes:
            first = 0 if l == top else a - 2 ** (l - 1)
            last = count if l == top else a + 2 ** (l - 1)
            self.covers[a] = (first // EIGHT, last // EIGHT)
        self.below = {
            a: [d for k, d in self.nodes if k < l
                and self.covers[a][0] <= self.covers[d][0] < self.covers[a][1]]
            for l, a in self.nodes
        }
        order = []
        for l, a in self.nodes:
            order += [(d, l) for d in self.below[a]] + [(a, 0)]
        self.high = {key: i for i, key in enumerate(order)}
        self.high_rhs = {a: i for i, (l, a) in enumerate(self.nodes)}
        self.blocks = max(top, len(self.mid), len(self.high))
        self.rhs = max(3, len(self.nodes))


def kernel(
    chips, count, plan,
    rhs_h, inv_h, pan_h, mask_s, irhs_h, iinv_h, ipan_h,
    leaf_out, inner_out,
    v_rhs, v_inv, v_pan, i_hi, i_lo, p_hi, p_lo, leaf_t,
    terms, terms_in, pieces1, pieces, upd,
    blocks, rblock, rhs_t, b_hi, b_lo,
    vin, win, wout, fwd, sol, solb, xhigh, full, leaf_acc, turned,
    in_sem, arr_sem, arr_rhs, put_send,
    ring_recv, ring_send, rring_recv, rring_send, sib_recv, sib_send, rsib_recv, rsib_send,
    t_recv, t_send, a1_recv, a1_send, a_recv, a_send,
    v_recv, v_send, w_recv, w_send, x_send, down_recv, down_send,
    ag_recv, ag_send, left_send, pair_recv, pair_send,
):
    top = pan_h.shape[0]
    width, nrhs = v_rhs.shape
    member = lax.axis_index("grp")
    j = lax.axis_index("row")
    z, c = lax.div(member, 2), lax.rem(member, 2)
    other = 1 - c
    parity = lax.rem(j, 2)
    place = lax.rem(j, EIGHT)
    group = lax.div(j, EIGHT)
    start = j - place
    host2 = start + 2
    odd, even = parity == 1, parity == 0
    is2 = place == 2
    is3 = j == plan.host3
    mate = jnp.where(odd, j - 1, j + 1)
    lev = jnp.int32(1)
    for bit in range(1, top):
        lev = lev + (lax.rem(j, 2**bit) == 0).astype(jnp.int32)
    nblocks = jnp.where(odd, top, jnp.where(is2, len(plan.mid), jnp.where(is3, len(plan.high), 0)))
    nlocal = jnp.where(odd, top, jnp.where(is2, plan.mid_local, 0))
    nnodes = jnp.where(odd, 1, jnp.where(is2, 3, jnp.where(is3, len(plan.nodes), 0)))
    nlocal_rhs = jnp.where(jnp.logical_or(odd, is2), 1, 0)

    def at(zz=None, cc=None, jj=None):
        zz = z if zz is None else zz
        cc = c if cc is None else cc
        return {"grp": zz * 2 + cc, "row": j if jj is None else jj}

    def turn(step):
        return lax.rem(z + step + chips, chips)

    def remote(src, dst, send, recv, where):
        return pltpu.make_async_remote_copy(
            src_ref=src, dst_ref=dst, send_sem=send, recv_sem=recv,
            device_id=where, device_id_type=pl.DeviceIdType.MESH,
        )

    def local(src, dst, sem):
        return pltpu.make_async_copy(src, dst, sem)

    def await_bytes(ref, sem):
        pltpu.make_async_copy(ref, ref, sem).wait()

    rhs_in = local(rhs_h, v_rhs, in_sem.at[top])
    inv_in = local(inv_h, v_inv, in_sem.at[top + 1])
    rhs_in.start()
    inv_in.start()

    def panel_in(step):
        return local(pan_h.at[step], v_pan.at[step], in_sem.at[step])

    panel_in(0).start()

    def keep(l, slot):
        src = iinv_h if l == 0 else ipan_h.at[l - 1]
        local(src, blocks.at[slot, z, c], arr_sem.at[slot]).start()

    @pl.when(odd)
    def _():
        for l in [0] + list(range(2, top + 1)):
            keep(l, max(l - 1, 0))

    @pl.when(is2)
    def _():
        for l in [0] + list(range(3, top + 1)):
            keep(l, plan.mid[2, l])

    @pl.when(jnp.logical_or(odd, is2))
    def _():
        local(irhs_h, rblock.at[0, z, c], arr_rhs.at[0]).start()

    for step in range(1, top):
        panel_in(step).start()

    barrier = pltpu.get_barrier_semaphore()

    def greet(where):
        pl.semaphore_signal(barrier, inc=1, device_id=where, device_id_type=pl.DeviceIdType.MESH)

    greet(at(cc=other))
    for step in range(1, chips):
        greet(at(zz=turn(step)))
    for step in range(chips):
        greet(at(zz=turn(step), jj=mate))

    @pl.when(is2)
    def _():
        for r in range(EIGHT):
            if r != 2:
                greet(at(jj=start + r))
        greet(at(jj=plan.host3))

    @pl.when(jnp.logical_not(is2))
    def _():
        greet(at(jj=host2))

    @pl.when(is3)
    def _():
        for g in range(plan.groups):
            greet(at(jj=g * EIGHT + 2))
        for l, a in plan.nodes:
            greet(at(jj=a))

    @pl.when(place == 0)
    def _():
        greet(at(jj=plan.host3))

    expected = 2 * chips + jnp.where(is2, EIGHT, 1)
    expected = expected + jnp.where(is3, plan.groups + len(plan.nodes), 0)
    expected = expected + jnp.where(place == 0, 1, 0)
    pl.semaphore_wait(barrier, expected)

    def puts(slots, rhs_slots, key, levels, target):
        for n, l in enumerate([0] + levels):
            src = iinv_h if l == 0 else ipan_h.at[l - 1]
            slot = slots[key, l]
            yield remote(
                src, blocks.at[slot, z, c], put_send.at[n], arr_sem.at[slot], at(jj=target)
            )
        slot = rhs_slots[key]
        yield remote(
            irhs_h, rblock.at[slot, z, c], put_send.at[top], arr_rhs.at[slot], at(jj=target)
        )

    def each_put(act):
        for key, l in ((6, 2), (4, 3)):
            @pl.when(place == key)
            def _(key=key, l=l):
                levels = list(range(l + 1, top + 1))
                for copy in puts(plan.mid, plan.mid_rhs, key, levels, host2):
                    act(copy)
        for l, a in plan.nodes:
            @pl.when(j == a)
            def _(l=l, a=a):
                levels = list(range(l + 1, top + 1))
                for copy in puts(plan.high, plan.high_rhs, a, levels, plan.host3):
                    act(copy)

    each_put(lambda copy: copy.start())

    right, left = chips // 2, chips - 1 - chips // 2

    def ring(buffer, send, recv, way, step, b):
        src = turn(-step if way == 0 else step)
        ref = buffer.at[b, src, c]
        target = turn(1 if way == 0 else -1)
        return remote(ref, ref, send.at[b], recv.at[way, step, b], at(zz=target))

    def ring_arrived(buffer, recv, way, step, b):
        src = turn(-step - 1 if way == 0 else step + 1)
        await_bytes(buffer.at[b, src, c], recv.at[way, step, b])

    kinds = (
        (blocks, arr_sem, ring_send, ring_recv, sib_send, sib_recv, nlocal, nblocks),
        (rblock, arr_rhs, rring_send, rring_recv, rsib_send, rsib_recv, nlocal_rhs, nnodes),
    )

    def first_step(near):
        for buffer, arrived, send, recv, _, _, mine, every in kinds:
            @pl.loop(0 if near else mine, mine if near else every)
            def _(b):
                await_bytes(buffer.at[b, z, c], arrived.at[b])
                if right:
                    ring(buffer, send, recv, 0, 0, b).start()
                if left:
                    ring(buffer, send, recv, 1, 0, b).start()

    def next_step(step):
        for buffer, _, send, recv, give, got, _, every in kinds:
            @pl.loop(0, every)
            def _(b):
                if step <= right:
                    ring_arrived(buffer, recv, 0, step - 1, b)
                    if step < right:
                        ring(buffer, send, recv, 0, step, b).start()
                if step <= left:
                    ring_arrived(buffer, recv, 1, step - 1, b)
                    if step < left:
                        ring(buffer, send, recv, 1, step, b).start()
                if step == max(right, left):
                    share(buffer, give, got, b).start()

    def share(buffer, send, recv, b):
        ref = buffer.at[b, :, c]
        return remote(ref, ref, send.at[b], recv.at[b], at(cc=other))

    def take_rhs(b):
        await_bytes(rblock.at[b, :, other], rsib_recv.at[b])
        rhs_t[b] = rblock[b].reshape(width, nrhs).T.reshape(rhs_t.shape[1:])

    def take_block(b):
        await_bytes(blocks.at[b, :, other], sib_recv.at[b])
        hi, lo = split(blocks[b].reshape(width, width))
        b_hi[b] = hi
        b_lo[b] = lo

    def block(b):
        return b_hi[b], b_lo[b]

    first_step(True)

    rhs_in.wait()
    inv_in.wait()
    hi, lo = split(v_inv[...])
    i_hi[...] = hi
    i_lo[...] = lo
    forward = product((hi, lo), split(v_rhs[...])).T
    leaf_t[...] = forward
    forward = split(forward)

    def swap_cores(l):
        return remote(
            terms.at[other, :, l], terms_in.at[:, l], t_send, t_recv.at[l], at(cc=other)
        )

    @pl.loop(0, top)
    def _(l):
        panel_in(l).wait()
        hi, lo = split(v_pan[l])
        p_hi[l] = hi
        p_lo[l] = lo
        term = product(forward, (hi, lo)) * mask_s[l].astype(F32)
        terms[:, :, l] = term.reshape(2, chips, -1, width)
        swap_cores(l).start()

    def add_cores(l):
        await_bytes(terms_in.at[:, l], t_recv.at[l])
        terms[c, :, l] = terms[c, :, l] + terms_in[:, l]

    def send_first(step):
        return remote(
            terms.at[c, turn(step), 0], pieces1.at[parity, z],
            a1_send.at[0 if step else 1], a1_recv.at[parity], at(zz=turn(step), jj=jnp.where(odd, j, mate)),
        )

    add_cores(0)

    @pl.when(even)
    def _():
        send_first(0).start()

    for step in range(1, chips):
        send_first(step).start()

    pl.loop(1, top)(add_cores)
    for step in range(1, chips):
        remote(
            terms.at[c, turn(step), 1:top], pieces.at[z], a_send, a_recv, at(zz=turn(step))
        ).start()

    first_step(False)
    for step in range(1, max(right, left)):
        next_step(step)

    @pl.when(odd)
    def _():
        next_step(max(right, left))

    def own_sum():
        await_bytes(pieces.at[0 : chips - 1], a_recv)
        total = terms[c, z, 1:top]
        for step in range(1, chips):
            total = total + pieces[turn(step)]
        upd[...] = total

    def send_v(l):
        return remote(
            upd.at[l - 2], vin.at[l - 2, place], v_send.at[l - 2], v_recv.at[l - 2], at(jj=host2)
        )

    @pl.when(even)
    def _():
        own_sum()

        @pl.when(is2)
        def _():
            vin[:, 2] = upd[...]

        @pl.when(jnp.logical_not(is2))
        def _():
            for l in range(2, top + 1):
                send_v(l).start()

        next_step(max(right, left))

    @pl.when(odd)
    def _():
        take_rhs(0)
        take_block(0)
        await_bytes(pieces1.at[0], a1_recv.at[0])
        await_bytes(pieces1.at[0, 0 : chips - 1], a1_recv.at[1])
        total = terms[c, z, 0] + pieces1[0, z]
        for step in range(1, chips):
            total = total + (pieces1[0, turn(step)] + pieces1[1, turn(step)])
        fwd[0] = thin(rhs_t[0, c, z] - total, block(0), NT)
        own_sum()

        @pl.loop(2, top + 1)
        def _(l):
            take_block(l - 1)
            upd[l - 2] = upd[l - 2] + thin(fwd[0], block(l - 1), NN)
            send_v(l).start()

    mid = plan.mid
    order = (1, 3, 5, 7, 0, 4, 6)

    def send_w(l):
        return remote(
            wout.at[l - 4], win.at[l - 4, group], w_send.at[l - 4], w_recv.at[l - 4],
            at(jj=plan.host3),
        )

    def arrived(l):
        await_bytes(vin.at[l - 2, 0 : EIGHT - 1], v_recv.at[l - 2])

    def slots(l, first, last):
        total = vin[l - 2, first]
        for r in range(first + 1, last):
            total = total + vin[l - 2, r]
        return total

    @pl.when(is2)
    def _():
        for b in range(3):
            take_rhs(b)
        pl.loop(0, len(mid))(take_block)
        arrived(2)
        fwd[0] = thin(rhs_t[0, c, z] - slots(2, 0, 4), block(mid[2, 0]), NT)
        fwd[1] = thin(rhs_t[1, c, z] - slots(2, 4, 8), block(mid[6, 0]), NT)
        arrived(3)
        fwd[2] = thin(
            rhs_t[2, c, z] - slots(3, 0, 8) - thin(fwd[0], block(mid[2, 3]), NN)
            - thin(fwd[1], block(mid[6, 3]), NN),
            block(mid[4, 0]), NT,
        )
        for l in range(4, top + 1):
            arrived(l)
            wout[l - 4] = slots(l, 0, 8) + (
                thin(fwd[0], block(mid[2, l]), NN) + thin(fwd[1], block(mid[6, l]), NN)
            ) + thin(fwd[2], block(mid[4, l]), NN)
            send_w(l).start()

    level_of = {a: l for l, a in plan.nodes}

    def send_x(a, g):
        n = plan.high_rhs[a]
        l = level_of[a]
        return remote(
            xhigh.at[n], sol.at[l - 1], x_send.at[n, g], down_recv.at[l - 1],
            at(jj=g * EIGHT + 2),
        )

    @pl.when(is3)
    def _():
        for b in range(len(plan.nodes)):
            take_rhs(b)
        pl.loop(0, len(plan.high))(take_block)
        for n, (l, a) in enumerate(plan.nodes):
            if n == 0 or plan.nodes[n - 1][0] != l:
                await_bytes(win.at[l - 4], w_recv.at[l - 4])
            total = rhs_t[n, c, z]
            for g in range(*plan.covers[a]):
                total = total - win[l - 4, g]
            for d in plan.below[a]:
                total = total - thin(fwd[plan.high_rhs[d]], block(plan.high[d, l]), NN)
            fwd[n] = thin(total, block(plan.high[a, 0]), NT)
        for l, a in reversed(plan.nodes):
            n = plan.high_rhs[a]
            rest = fwd[n]
            for k, up in plan.nodes:
                if a in plan.below[up]:
                    rest = rest - thin(xhigh[plan.high_rhs[up]], block(plan.high[a, k]), NT)
            xhigh[n] = thin(rest, block(plan.high[a, 0]), NN)
            for g in range(*plan.covers[a]):
                send_x(a, g).start()

    leaf_acc[...] = jnp.zeros_like(leaf_acc)

    def send_down(l, r, src=None):
        src = sol.at[l - 1] if src is None else src
        return remote(
            src, sol.at[l - 1], down_send.at[l - 1], down_recv.at[l - 1], at(jj=start + r)
        )

    def spread(l):
        full[l - 1, c, z] = sol[l - 1]
        for step in range(1, chips):
            remote(
                sol.at[l - 1], full.at[l - 1, c, z], ag_send.at[l - 1], ag_recv.at[l - 1],
                at(zz=turn(step)),
            ).start()

    def spread_left(step):
        return remote(
            sol.at[0], full.at[0, c, z], left_send, ag_recv.at[0], at(zz=turn(step), jj=mate)
        )

    @pl.when(is2)
    def _():
        rest = [fwd[0], fwd[1], fwd[2]]
        for l in range(top, 3, -1):
            await_bytes(sol.at[l - 1], down_recv.at[l - 1])
            for r in order:
                send_down(l, r).start()
            for n, key in enumerate((2, 6, 4)):
                rest[n] = rest[n] - thin(sol[l - 1], block(mid[key, l]), NT)
        sol[2] = thin(rest[2], block(mid[4, 0]), NN)
        for r in order:
            send_down(3, r).start()
        for n, key in enumerate((2, 6)):
            rest[n] = rest[n] - thin(sol[2], block(mid[key, 3]), NT)
        sol[1] = thin(rest[0], block(mid[2, 0]), NN)
        solb[...] = thin(rest[1], block(mid[6, 0]), NN)
        for r in order:
            send_down(2, r, None if r < 4 else solb).start()
        for l in range(top, 1, -1):
            spread(l)

    @pl.when(odd)
    def _():
        rest = fwd[0]
        for l in range(top, 1, -1):
            await_bytes(sol.at[l - 1], down_recv.at[l - 1])
            rest = rest - thin(sol[l - 1], block(l - 1), NT)
            if l > 3:
                spread(l)
        sol[0] = thin(rest, block(0), NN)
        spread(1)
        for step in range(chips):
            spread_left(step).start()
        for l in (3, 2):
            spread(l)

    @pl.when(jnp.logical_and(even, jnp.logical_not(is2)))
    def _():
        for l in range(top, 1, -1):
            await_bytes(sol.at[l - 1], down_recv.at[l - 1])
            spread(l)

    def pair(l):
        return remote(full.at[l, c], full.at[l, c], pair_send.at[l], pair_recv.at[l], at(cc=other))

    def leaf_back(l):
        await_bytes(full.at[l, other], pair_recv.at[l])
        ancestor = split(full[l].reshape(nrhs, width))
        leaf_acc[...] = leaf_acc[...] + mask_s[l].astype(F32) * product(
            ancestor, (p_hi[l], p_lo[l]), NT
        )

    @pl.loop(0, top)
    def _(i):
        l = top - 1 - i

        @pl.when(jnp.logical_and(l == 0, even))
        def _():
            await_bytes(full.at[0, c], ag_recv.at[0])

        @pl.when(jnp.logical_or(l > 0, odd))
        def _():
            await_bytes(full.at[l, c, 0 : chips - 1], ag_recv.at[l])

        pair(l).start()

        @pl.when(i >= 1)
        def _():
            leaf_back(l + 1)

    leaf_back(0)
    rest = split(leaf_t[...] - leaf_acc[...])
    leaf_out[...] = product(rest, (i_hi[...], i_lo[...])).T
    share_rows = inner_out.shape[0]
    turned[...] = full[lev - 1].reshape(nrhs, width).T
    inner_out[...] = turned[pl.ds(pl.multiple_of(member * share_rows, share_rows), share_rows), :]

    each_put(lambda copy: copy.wait_send())
    for buffer, _, send, _, give, _, _, every in kinds:
        @pl.loop(0, every)
        def _(b):
            await_bytes(buffer.at[b, 0 : chips - 1, 0], send.at[b])
            await_bytes(buffer.at[b, :, c], give.at[b])
    await_bytes(terms.at[0], t_send)
    await_bytes(pieces1.at[0, 0 : chips - 1], a1_send.at[0])
    await_bytes(pieces.at[0 : chips - 1], a_send)

    @pl.when(jnp.logical_not(is2))
    def _():
        for l in range(2, top + 1):
            send_v(l).wait_send()

    @pl.when(is2)
    def _():
        for l in range(4, top + 1):
            send_w(l).wait_send()
        for l in range(2, top + 1):
            await_bytes(vin.at[0, 0 : EIGHT - 1], down_send.at[l - 1])

    @pl.when(is3)
    def _():
        for l, a in plan.nodes:
            for g in range(*plan.covers[a]):
                send_x(a, g).wait_send()

    @pl.loop(1, top)
    def _(l):
        await_bytes(full.at[l, 0, 0 : chips - 1], ag_send.at[l])

    @pl.when(odd)
    def _():
        await_bytes(full.at[0, 0, 0 : chips - 1], ag_send.at[0])
        await_bytes(full.at[0, 0], left_send)

    @pl.when(even)
    def _():
        send_first(0).wait_send()

    @pl.loop(0, top)
    def _(l):
        pair(l).wait_send()


def per_device(leaf_rhs, leaf_inv, leaf_panel, leaf_mask, inner_rhs, inner_inv, inner_panel):
    members, count = lax.axis_size("grp"), lax.axis_size("row")
    chips = members // 2
    width, nrhs = leaf_rhs.shape[2:]
    top = leaf_panel.shape[2]
    share, cols = width // members, nrhs // members
    plan = Plan(top, count)
    nb, nr, high = plan.blocks, plan.rhs, top - 3
    hbm = pl.BlockSpec(memory_space=pl.ANY)
    dma = pltpu.SemaphoreType.DMA
    steps = max(chips // 2, 1)
    v = pltpu.VMEM
    call = pl.pallas_call(
        functools.partial(kernel, chips, count, plan),
        out_shape=(
            jax.ShapeDtypeStruct((width, nrhs), F32),
            jax.ShapeDtypeStruct((share, nrhs), F32),
        ),
        in_specs=[hbm, hbm, hbm, pl.BlockSpec(memory_space=pltpu.SMEM), hbm, hbm, hbm],
        out_specs=[pl.BlockSpec(memory_space=pltpu.VMEM)] * 2,
        scratch_shapes=[
            v((width, nrhs), F32),
            v((width, width), F32),
            v((top, width, width), F32),
            v((width, width), BF16),
            v((width, width), BF16),
            v((top, width, width), BF16),
            v((top, width, width), BF16),
            v((nrhs, width), F32),
            v((2, chips, top, cols, width), F32),
            v((chips, top, cols, width), F32),
            v((2, chips, cols, width), F32),
            v((chips, top - 1, cols, width), F32),
            v((top - 1, cols, width), F32),
            v((nb, chips, 2, share, width), F32),
            v((nr, chips, 2, share, nrhs), F32),
            v((nr, 2, chips, cols, width), F32),
            v((nb, width, width), BF16),
            v((nb, width, width), BF16),
            v((top - 1, EIGHT, cols, width), F32),
            v((high, plan.groups, cols, width), F32),
            v((high, cols, width), F32),
            v((nr, cols, width), F32),
            v((top, cols, width), F32),
            v((cols, width), F32),
            v((len(plan.nodes), cols, width), F32),
            v((top, 2, chips, cols, width), F32),
            v((nrhs, width), F32),
            v((width, nrhs), F32),
            dma((top + 2,)),
            dma((nb,)),
            dma((nr,)),
            dma((top + 1,)),
            dma((2, steps, nb)),
            dma((nb,)),
            dma((2, steps, nr)),
            dma((nr,)),
            dma((nb,)),
            dma((nb,)),
            dma((nr,)),
            dma((nr,)),
            dma((top,)),
            dma,
            dma((2,)),
            dma((2,)),
            dma,
            dma,
            dma((top - 1,)),
            dma((top - 1,)),
            dma((high,)),
            dma((high,)),
            dma((len(plan.nodes), plan.groups)),
            dma((top,)),
            dma((top,)),
            dma((top,)),
            dma((top,)),
            dma,
            dma((top,)),
            dma((top,)),
        ],
        compiler_params=pltpu.CompilerParams(
            collective_id=0, has_side_effects=True, vmem_limit_bytes=60 * 2**20
        ),
    )
    leaf, inner = call(
        leaf_rhs[0, 0], leaf_inv[0, 0], leaf_panel[0, 0], leaf_mask[0, 0],
        inner_rhs[0], inner_inv[0], inner_panel[0],
    )
    return leaf[None, None], inner[None]


def solution(mesh):
    in_specs = (
        P("row", "grp", None, None),
        P("row", "grp", None, None),
        P("row", "grp", None, None, None),
        P("row", "grp", None),
        P("row", "grp", None),
        P("row", "grp", None),
        P("row", None, "grp", None),
    )
    out_specs = (P("row", "grp", None, None), P("row", "grp", None))
    return jax.shard_map(
        per_device, mesh=mesh, in_specs=in_specs, out_specs=out_specs, check_vma=False
    )
```

```python
import functools

import jax
import jax.numpy as jnp
from jax import lax
from jax.experimental import pallas as pl
from jax.experimental.pallas import tpu as pltpu
from jax.sharding import PartitionSpec as P

F32 = jnp.float32
BF16 = jnp.bfloat16
NN = (((1,), (0,)), ((), ()))
NT = (((1,), (1,)), ((), ()))
EIGHT = 8


def split(x):
    high = x.astype(BF16)
    return high, (x - high.astype(F32)).astype(BF16)


def dot(a, b, dims):
    return lax.dot_general(a, b, dims, preferred_element_type=F32)


def product(a, b, dims=NN):
    return dot(a[0], b[0], dims) + (dot(a[0], b[1], dims) + dot(a[1], b[0], dims))


def thin(x, w, dims):
    rows = x.shape[0]
    high = x.astype(BF16).astype(F32)
    both = jnp.concatenate([high, x - high], axis=0).astype(BF16)
    first, second = dot(both, w[0], dims), dot(both, w[1], dims)
    return first[:rows] + (first[rows:] + second[:rows])


class Plan:
    def __init__(self, top, count):
        self.groups = count // EIGHT
        self.host3 = 12 if count > EIGHT else 4
        order = [(key, l) for key in (2, 6) for l in [0] + list(range(3, top + 1))]
        order += [(4, l) for l in [0] + list(range(4, top + 1))]
        self.mid = {key: i for i, key in enumerate(order)}
        self.mid_rhs = {2: 0, 6: 1, 4: 2}
        self.items = [(0, 2, 0, 4), (7, 2, 4, 4)]
        for place, l in zip((6, 1, 5, 3), range(3, top + 1)):
            self.items.append((place, l, 0, EIGHT))
        self.nodes = []
        for l in range(4, top):
            self.nodes += [(l, a) for a in range(2 ** (l - 1), count, 2**l)]
        self.nodes.append((top, 0))
        self.covers = {}
        for l, a in self.nodes:
            first = 0 if l == top else a - 2 ** (l - 1)
            last = count if l == top else a + 2 ** (l - 1)
            self.covers[a] = (first // EIGHT, last // EIGHT)
        self.below = {
            a: [d for k, d in self.nodes if k < l
                and self.covers[a][0] <= self.covers[d][0] < self.covers[a][1]]
            for l, a in self.nodes
        }
        order = []
        for l, a in self.nodes:
            order += [(d, l) for d in self.below[a]] + [(a, 0)]
        self.blocks = len(self.mid) + len(order)
        self.high = {key: len(self.mid) + i for i, key in enumerate(order)}
        self.rhs = 3 + len(self.nodes)
        self.high_rhs = {a: 3 + i for i, (l, a) in enumerate(self.nodes)}


def kernel(
    chips, count, plan,
    rhs_h, inv_h, pan_h, mask_s, irhs_h, iinv_h, ipan_h,
    leaf_out, inner_out,
    v_rhs, v_inv, v_pan, i_hi, i_lo, p_hi, p_lo, leaf_t,
    terms, terms_in, pieces1, upd,
    gather, gsum, gchips, gout, tin,
    blocks, rblock, rhs_t, b_hi, b_lo,
    vin, win, wout, fwd, sol, solb, xhigh, full, leaf_acc, turned,
    in_sem, arr_sem, arr_rhs, put_send,
    ring_recv, ring_send, rring_recv, rring_send, sib_recv, sib_send, rsib_recv, rsib_send,
    fw_recv, fw_send, rfw_recv, rfw_send,
    t_recv, t_send, a1_recv, a1_send,
    g_recv, g_send, gz_recv, gz_send, tin_recv, tin_send,
    v_recv, v_send, w_recv, w_send, x_send, down_recv, down_send,
    ag_recv, ag_send, left_send, pair_recv, pair_send,
):
    top = pan_h.shape[0]
    width, nrhs = v_rhs.shape
    member = lax.axis_index("grp")
    j = lax.axis_index("row")
    z, c = lax.div(member, 2), lax.rem(member, 2)
    other = 1 - c
    parity = lax.rem(j, 2)
    place = lax.rem(j, EIGHT)
    group = lax.div(j, EIGHT)
    start = j - place
    host2 = start + 2
    odd, even = parity == 1, parity == 0
    is2 = place == 2
    is3 = j == plan.host3
    mate = jnp.where(odd, j - 1, j + 1)
    lev = jnp.int32(1)
    for bit in range(1, top):
        lev = lev + (lax.rem(j, 2**bit) == 0).astype(jnp.int32)
    is0, is6 = place == 0, place == 6
    helps = jnp.logical_or(is0, is6)
    near = jnp.logical_not(jnp.logical_or(is0, place == 4))
    low = jnp.where(is6, top - 1, jnp.where(is0, 2 * (top - 1), 0))
    size = jnp.where(odd, top, jnp.where(is0, top - 2, top - 1))
    size = jnp.where(place == 4, 0, size)
    rlow = jnp.where(is6, 1, jnp.where(is0, 2, 0))
    rsize = jnp.where(place == 4, 0, 1)
    nmid = len(plan.mid)

    def at(zz=None, cc=None, jj=None):
        zz = z if zz is None else zz
        cc = c if cc is None else cc
        return {"grp": zz * 2 + cc, "row": j if jj is None else jj}

    def turn(step):
        return lax.rem(z + step + chips, chips)

    def remote(src, dst, send, recv, where):
        return pltpu.make_async_remote_copy(
            src_ref=src, dst_ref=dst, send_sem=send, recv_sem=recv,
            device_id=where, device_id_type=pl.DeviceIdType.MESH,
        )

    def local(src, dst, sem):
        return pltpu.make_async_copy(src, dst, sem)

    def await_bytes(ref, sem):
        pltpu.make_async_copy(ref, ref, sem).wait()

    rhs_in = local(rhs_h, v_rhs, in_sem.at[top])
    inv_in = local(inv_h, v_inv, in_sem.at[top + 1])
    rhs_in.start()
    inv_in.start()

    def panel_in(step):
        return local(pan_h.at[step], v_pan.at[step], in_sem.at[step])

    panel_in(0).start()

    def keep(l, slot):
        src = iinv_h if l == 0 else ipan_h.at[l - 1]
        local(src, blocks.at[slot, z, c], arr_sem.at[slot]).start()

    @pl.when(odd)
    def _():
        for l in [0] + list(range(2, top + 1)):
            keep(l, max(l - 1, 0))

    for key in (2, 6):
        @pl.when(place == key)
        def _(key=key):
            for l in [0] + list(range(3, top + 1)):
                keep(l, plan.mid[key, l])

    @pl.when(near)
    def _():
        local(irhs_h, rblock.at[rlow, z, c], arr_rhs.at[rlow]).start()

    for step in range(1, top):
        panel_in(step).start()

    barrier = pltpu.get_barrier_semaphore()

    def greet(where):
        pl.semaphore_signal(barrier, inc=1, device_id=where, device_id_type=pl.DeviceIdType.MESH)

    greet(at(cc=other))
    for step in range(1, chips):
        greet(at(zz=turn(step)))
    for step in range(chips):
        greet(at(zz=turn(step), jj=mate))

    for step in range(1, EIGHT):
        greet(at(jj=start + lax.rem(place + step, EIGHT)))

    @pl.when(is2)
    def _():
        greet(at(jj=plan.host3))

    @pl.when(is3)
    def _():
        for g in range(plan.groups):
            greet(at(jj=g * EIGHT + 2))
        for l, a in plan.nodes:
            greet(at(jj=a))

    @pl.when(is0)
    def _():
        greet(at(jj=plan.host3))

    expected = 2 * chips + EIGHT - 1 + jnp.where(is2, 1, 0) + jnp.where(is0, 1, 0)
    expected = expected + jnp.where(is3, plan.groups + len(plan.nodes), 0)

    def puts(slots, rhs_slots, key, levels, target):
        for n, l in enumerate([0] + levels):
            src = iinv_h if l == 0 else ipan_h.at[l - 1]
            slot = slots[key, l]
            yield remote(
                src, blocks.at[slot, z, c], put_send.at[n], arr_sem.at[slot], at(jj=target)
            )
        slot = rhs_slots[key]
        yield remote(
            irhs_h, rblock.at[slot, z, c], put_send.at[top], arr_rhs.at[slot], at(jj=target)
        )

    def each_put(act):
        @pl.when(place == 4)
        def _():
            for copy in puts(plan.mid, plan.mid_rhs, 4, list(range(4, top + 1)), start):
                act(copy)
        for l, a in plan.nodes:
            @pl.when(j == a)
            def _(l=l, a=a):
                levels = list(range(l + 1, top + 1))
                for copy in puts(plan.high, plan.high_rhs, a, levels, plan.host3):
                    act(copy)

    right, left = chips // 2, chips - 1 - chips // 2

    def heading(way, b):
        return (1 if way == 0 else -1) * (1 - 2 * lax.rem(b, 2))

    def ring(kind, way, step, b):
        ref = kind[0].at[b, turn(-step * heading(way, b)), c]
        return remote(
            ref, ref, kind[2].at[b], kind[3].at[way, step, b], at(zz=turn(heading(way, b)))
        )

    def ring_arrived(kind, way, step, b):
        src = turn(-(step + 1) * heading(way, b))
        await_bytes(kind[0].at[b, src, c], kind[3].at[way, step, b])
        pass_on(kind, b, src)

    kinds = (
        (blocks, arr_sem, ring_send, ring_recv, sib_send, sib_recv, fw_send, fw_recv),
        (rblock, arr_rhs, rring_send, rring_recv, rsib_send, rsib_recv, rfw_send, rfw_recv),
    )
    ranges = ((low, low + size), (rlow, rlow + rsize))
    ranges3 = (
        (nmid, jnp.where(is3, plan.blocks, nmid)),
        (3, jnp.where(is3, plan.rhs, 3)),
    )

    def pass_on(kind, b, src):
        @pl.when(passes(kind, b))
        def _():
            ref = kind[0].at[b, src, c]
            remote(ref, ref, kind[6].at[b], kind[7].at[b], at(jj=host2)).start()

    def first_step(ranges):
        for kind, (first, last) in zip(kinds, ranges):
            @pl.loop(first, last)
            def _(b):
                await_bytes(kind[0].at[b, z, c], kind[1].at[b])
                if right:
                    ring(kind, 0, 0, b).start()
                if left:
                    ring(kind, 1, 0, b).start()
                pass_on(kind, b, z)

    final = max(right, left)

    def next_step(step, ranges):
        for kind, (first, last) in zip(kinds, ranges):
            @pl.loop(first, last)
            def _(b):
                if step <= right:
                    ring_arrived(kind, 0, step - 1, b)
                    if step < right:
                        ring(kind, 0, step, b).start()
                if step <= left:
                    ring_arrived(kind, 1, step - 1, b)
                    if step < left:
                        ring(kind, 1, step, b).start()
                if step == final:
                    @pl.when(jnp.logical_not(passes(kind, b)))
                    def _():
                        share(kind, b).start()

    def passes(kind, b):
        return jnp.logical_and(helps, b < (nmid if kind[0] is blocks else 3))

    def share(kind, b):
        ref = kind[0].at[b, :, c]
        return remote(ref, ref, kind[4].at[b], kind[5].at[b], at(cc=other))

    def helped(kind, first, last):
        @pl.loop(first, last)
        def _(b):
            await_bytes(kind[0].at[b, :, c], kind[7].at[b])
            share(kind, b).start()

    def take_rhs(b):
        await_bytes(rblock.at[b, :, other], rsib_recv.at[b])
        rhs_t[b] = rblock[b].reshape(width, nrhs).T.reshape(rhs_t.shape[1:])

    def take_block(b):
        await_bytes(blocks.at[b, :, other], sib_recv.at[b])
        hi, lo = split(blocks[b].reshape(width, width))
        b_hi[b] = hi
        b_lo[b] = lo

    def block(b):
        return b_hi[b], b_lo[b]

    rhs_in.wait()
    inv_in.wait()
    hi, lo = split(v_inv[...])
    i_hi[...] = hi
    i_lo[...] = lo
    forward = product((hi, lo), split(v_rhs[...])).T
    leaf_t[...] = forward
    forward = split(forward)

    def swap_cores(l):
        return remote(
            terms.at[other, :, l], terms_in.at[:, l], t_send, t_recv.at[l], at(cc=other)
        )

    @pl.loop(0, top)
    def _(l):
        panel_in(l).wait()
        hi, lo = split(v_pan[l])
        p_hi[l] = hi
        p_lo[l] = lo
        term = product(forward, (hi, lo)) * mask_s[l].astype(F32)
        terms[:, :, l] = term.reshape(2, chips, -1, width)

    pl.semaphore_wait(barrier, expected)

    for l in range(top):
        swap_cores(l).start()
    each_put(lambda copy: copy.start())
    nowhere = lambda pair: (pair[0], jnp.where(near, pair[1], pair[0]))
    first_step([nowhere(pair) for pair in ranges])

    def add_cores(l):
        await_bytes(terms_in.at[:, l], t_recv.at[l])
        terms[c, :, l] = terms[c, :, l] + terms_in[:, l]

    def send_first(step):
        return remote(
            terms.at[c, turn(step), 0], pieces1.at[parity, z],
            a1_send.at[0 if step else 1], a1_recv.at[parity], at(zz=turn(step), jj=jnp.where(odd, j, mate)),
        )

    add_cores(0)

    @pl.when(even)
    def _():
        send_first(0).start()

    for step in range(1, chips):
        send_first(step).start()

    def collect(i):
        at_place, l, first, n = plan.items[i]
        return remote(
            terms.at[c, :, l - 1], gather.at[place], g_send.at[i], g_recv, at(jj=start + at_place)
        )

    def each_collect(l, act):
        for i, (at_place, level, first, n) in enumerate(plan.items):
            if level == l:
                @pl.when(jnp.logical_and(
                    place != at_place, jnp.logical_and(place >= first, place < first + n)
                ))
                def _(i=i):
                    act(collect(i))

    for l in range(2, top + 1):
        add_cores(l - 1)
        each_collect(l, lambda copy: copy.start())

    holds, my_item, my_level = place < 0, jnp.int32(0), jnp.int32(0)
    for i, (at_place, l, first, n) in enumerate(plan.items):
        mine = place == at_place
        holds = jnp.logical_or(holds, mine)
        my_item = jnp.where(mine, i, my_item)
        my_level = jnp.where(mine, l - 1, my_level)
    sources = jnp.where(my_item < 2, 4, EIGHT)
    origin = jnp.where(my_item == 1, 4, 0)

    def to_chip(step):
        return remote(gsum.at[turn(step)], gchips.at[z], gz_send, gz_recv, at(zz=turn(step)))

    def to_host():
        return remote(gout, tin.at[my_item], tin_send, tin_recv.at[my_item], at(jj=host2))

    def sum_places():
        @pl.when(holds)
        def _():
            @pl.when(my_item < 2)
            def _():
                await_bytes(gather.at[0:3], g_recv)

            @pl.when(my_item >= 2)
            def _():
                await_bytes(gather.at[0 : EIGHT - 1], g_recv)

            gsum[...] = terms[c, :, my_level]

            @pl.loop(1, sources)
            def _(k):
                r = origin + lax.rem(place - origin + k, sources)
                gsum[...] = gsum[...] + gather[r]

            for step in range(1, chips):
                to_chip(step).start()

    def sum_chips():
        @pl.when(holds)
        def _():
            await_bytes(gchips.at[0 : chips - 1], gz_recv)
            total = gsum[z]
            for step in range(1, chips):
                total = total + gchips[turn(step)]
            gout[...] = total
            to_host().start()

    far = lambda pair: (pair[0], jnp.where(near, pair[0], pair[1]))
    first_step([far(pair) for pair in ranges])
    first_step(ranges3)
    between = (final + 1) // 2
    for step in range(1, final + 1):
        next_step(step, ranges)
        next_step(step, ranges3)
        if step == between:
            sum_places()
    sum_chips()

    def send_v(l):
        return remote(
            upd.at[l - 2], vin.at[l - 2, lax.div(place, 2)], v_send.at[l - 2], v_recv.at[l - 2],
            at(jj=host2),
        )

    @pl.when(odd)
    def _():
        take_rhs(0)
        take_block(0)
        await_bytes(pieces1.at[0], a1_recv.at[0])
        await_bytes(pieces1.at[0, 0 : chips - 1], a1_recv.at[1])
        total = terms[c, z, 0] + pieces1[0, z]
        for step in range(1, chips):
            total = total + (pieces1[0, turn(step)] + pieces1[1, turn(step)])
        fwd[0] = thin(rhs_t[0, c, z] - total, block(0), NT)
        @pl.loop(2, top + 1)
        def _(l):
            take_block(l - 1)
            upd[l - 2] = thin(fwd[0], block(l - 1), NN)
            send_v(l).start()

    mid = plan.mid
    order = (1, 3, 5, 7, 0, 4, 6)

    def send_w(l):
        return remote(
            wout.at[l - 4], win.at[l - 4, group], w_send.at[l - 4], w_recv.at[l - 4],
            at(jj=plan.host3),
        )

    def arrived(l):
        await_bytes(vin.at[l - 2], v_recv.at[l - 2])
        for i, item in enumerate(plan.items):
            if item[1] == l:
                await_bytes(tin.at[i], tin_recv.at[i])

    def slots(l, first, last):
        total = tin[l - 1 if l > 2 else first // 2]
        for r in range(first, last):
            total = total + vin[l - 2, r]
        return total

    @pl.when(is2)
    def _():
        helped(kinds[1], 1, 3)
        helped(kinds[0], top - 1, nmid)
        for b in range(3):
            take_rhs(b)
        pl.loop(0, nmid)(take_block)
        arrived(2)
        fwd[0] = thin(rhs_t[0, c, z] - slots(2, 0, 2), block(mid[2, 0]), NT)
        fwd[1] = thin(rhs_t[1, c, z] - slots(2, 2, 4), block(mid[6, 0]), NT)
        arrived(3)
        fwd[2] = thin(
            rhs_t[2, c, z] - slots(3, 0, 4) - thin(fwd[0], block(mid[2, 3]), NN)
            - thin(fwd[1], block(mid[6, 3]), NN),
            block(mid[4, 0]), NT,
        )
        for l in range(4, top + 1):
            arrived(l)
            wout[l - 4] = slots(l, 0, 4) + (
                thin(fwd[0], block(mid[2, l]), NN) + thin(fwd[1], block(mid[6, l]), NN)
            ) + thin(fwd[2], block(mid[4, l]), NN)
            send_w(l).start()

    level_of = {a: l for l, a in plan.nodes}

    def send_x(a, g):
        n = plan.high_rhs[a] - 3
        l = level_of[a]
        return remote(
            xhigh.at[n], sol.at[l - 1], x_send.at[n, g], down_recv.at[l - 1],
            at(jj=g * EIGHT + 2),
        )

    @pl.when(is3)
    def _():
        for b in range(3, plan.rhs):
            take_rhs(b)
        pl.loop(nmid, plan.blocks)(take_block)
        for n, (l, a) in enumerate(plan.nodes):
            if n == 0 or plan.nodes[n - 1][0] != l:
                await_bytes(win.at[l - 4], w_recv.at[l - 4])
            total = rhs_t[3 + n, c, z]
            for g in range(*plan.covers[a]):
                total = total - win[l - 4, g]
            for d in plan.below[a]:
                total = total - thin(fwd[plan.high_rhs[d] - 3], block(plan.high[d, l]), NN)
            fwd[n] = thin(total, block(plan.high[a, 0]), NT)
        for l, a in reversed(plan.nodes):
            n = plan.high_rhs[a] - 3
            rest = fwd[n]
            for k, up in plan.nodes:
                if a in plan.below[up]:
                    rest = rest - thin(xhigh[plan.high_rhs[up] - 3], block(plan.high[a, k]), NT)
            xhigh[n] = thin(rest, block(plan.high[a, 0]), NN)
            for g in range(*plan.covers[a]):
                send_x(a, g).start()

    leaf_acc[...] = jnp.zeros_like(leaf_acc)

    def send_down(l, r, src=None):
        src = sol.at[l - 1] if src is None else src
        return remote(
            src, sol.at[l - 1], down_send.at[l - 1], down_recv.at[l - 1], at(jj=start + r)
        )

    def spread(l):
        full[l - 1, c, z] = sol[l - 1]
        for step in range(1, chips):
            remote(
                sol.at[l - 1], full.at[l - 1, c, z], ag_send.at[l - 1], ag_recv.at[l - 1],
                at(zz=turn(step)),
            ).start()

    def spread_left(step):
        return remote(
            sol.at[0], full.at[0, c, z], left_send, ag_recv.at[0], at(zz=turn(step), jj=mate)
        )

    @pl.when(is2)
    def _():
        rest = [fwd[0], fwd[1], fwd[2]]
        for l in range(top, 3, -1):
            await_bytes(sol.at[l - 1], down_recv.at[l - 1])
            for r in order:
                send_down(l, r).start()
            for n, key in enumerate((2, 6, 4)):
                rest[n] = rest[n] - thin(sol[l - 1], block(mid[key, l]), NT)
        sol[2] = thin(rest[2], block(mid[4, 0]), NN)
        for r in order:
            send_down(3, r).start()
        for n, key in enumerate((2, 6)):
            rest[n] = rest[n] - thin(sol[2], block(mid[key, 3]), NT)
        sol[1] = thin(rest[0], block(mid[2, 0]), NN)
        solb[...] = thin(rest[1], block(mid[6, 0]), NN)
        for r in order:
            send_down(2, r, None if r < 4 else solb).start()
        for l in range(top, 1, -1):
            spread(l)

    @pl.when(odd)
    def _():
        rest = fwd[0]
        for l in range(top, 1, -1):
            await_bytes(sol.at[l - 1], down_recv.at[l - 1])
            rest = rest - thin(sol[l - 1], block(l - 1), NT)
            if l > 3:
                spread(l)
        sol[0] = thin(rest, block(0), NN)
        spread(1)
        for step in range(chips):
            spread_left(step).start()
        for l in (3, 2):
            spread(l)

    @pl.when(jnp.logical_and(even, jnp.logical_not(is2)))
    def _():
        for l in range(top, 1, -1):
            await_bytes(sol.at[l - 1], down_recv.at[l - 1])
            spread(l)

    def pair(l):
        return remote(full.at[l, c], full.at[l, c], pair_send.at[l], pair_recv.at[l], at(cc=other))

    def leaf_back(l):
        await_bytes(full.at[l, other], pair_recv.at[l])
        ancestor = split(full[l].reshape(nrhs, width))
        leaf_acc[...] = leaf_acc[...] + mask_s[l].astype(F32) * product(
            ancestor, (p_hi[l], p_lo[l]), NT
        )

    @pl.loop(0, top)
    def _(i):
        l = top - 1 - i

        @pl.when(jnp.logical_and(l == 0, even))
        def _():
            await_bytes(full.at[0, c], ag_recv.at[0])

        @pl.when(jnp.logical_or(l > 0, odd))
        def _():
            await_bytes(full.at[l, c, 0 : chips - 1], ag_recv.at[l])

        pair(l).start()

        @pl.when(i >= 1)
        def _():
            leaf_back(l + 1)

    leaf_back(0)
    rest = split(leaf_t[...] - leaf_acc[...])
    leaf_out[...] = product(rest, (i_hi[...], i_lo[...])).T
    share_rows = inner_out.shape[0]
    turned[...] = full[lev - 1].reshape(nrhs, width).T
    inner_out[...] = turned[pl.ds(pl.multiple_of(member * share_rows, share_rows), share_rows), :]

    each_put(lambda copy: copy.wait_send())
    for some in (ranges, ranges3):
        for kind, (first, last) in zip(kinds, some):
            @pl.loop(first, last)
            def _(b):
                await_bytes(kind[0].at[b, 0 : chips - 1, 0], kind[2].at[b])
                gone = jnp.where(passes(kind, b), 1, 0)

                @pl.when(gone == 1)
                def _():
                    await_bytes(kind[0].at[b, :, c], kind[6].at[b])

                @pl.when(gone == 0)
                def _():
                    await_bytes(kind[0].at[b, :, c], kind[4].at[b])

    @pl.when(is2)
    def _():
        for kind, (first, last) in zip(kinds, ((top - 1, nmid), (1, 3))):
            @pl.loop(first, last)
            def _(b):
                await_bytes(kind[0].at[b, :, c], kind[4].at[b])
    await_bytes(terms.at[0], t_send)
    await_bytes(pieces1.at[0, 0 : chips - 1], a1_send.at[0])
    for l in range(2, top + 1):
        each_collect(l, lambda copy: copy.wait_send())

    @pl.when(holds)
    def _():
        await_bytes(gchips.at[0 : chips - 1], gz_send)
        to_host().wait_send()

    @pl.when(odd)
    def _():
        for l in range(2, top + 1):
            send_v(l).wait_send()

    @pl.when(is2)
    def _():
        for l in range(4, top + 1):
            send_w(l).wait_send()
        for l in range(2, top + 1):
            await_bytes(gather.at[0 : EIGHT - 1, 0], down_send.at[l - 1])

    @pl.when(is3)
    def _():
        for l, a in plan.nodes:
            for g in range(*plan.covers[a]):
                send_x(a, g).wait_send()

    @pl.loop(1, top)
    def _(l):
        await_bytes(full.at[l, 0, 0 : chips - 1], ag_send.at[l])

    @pl.when(odd)
    def _():
        await_bytes(full.at[0, 0, 0 : chips - 1], ag_send.at[0])
        await_bytes(full.at[0, 0], left_send)

    @pl.when(even)
    def _():
        send_first(0).wait_send()

    @pl.loop(0, top)
    def _(l):
        pair(l).wait_send()


def per_device(leaf_rhs, leaf_inv, leaf_panel, leaf_mask, inner_rhs, inner_inv, inner_panel):
    members, count = lax.axis_size("grp"), lax.axis_size("row")
    chips = members // 2
    width, nrhs = leaf_rhs.shape[2:]
    top = leaf_panel.shape[2]
    share, cols = width // members, nrhs // members
    plan = Plan(top, count)
    nb, nr, high = plan.blocks, plan.rhs, top - 3
    hbm = pl.BlockSpec(memory_space=pl.ANY)
    dma = pltpu.SemaphoreType.DMA
    steps = max(chips // 2, 1)
    v = pltpu.VMEM
    call = pl.pallas_call(
        functools.partial(kernel, chips, count, plan),
        out_shape=(
            jax.ShapeDtypeStruct((width, nrhs), F32),
            jax.ShapeDtypeStruct((share, nrhs), F32),
        ),
        in_specs=[hbm, hbm, hbm, pl.BlockSpec(memory_space=pltpu.SMEM), hbm, hbm, hbm],
        out_specs=[pl.BlockSpec(memory_space=pltpu.VMEM)] * 2,
        scratch_shapes=[
            v((width, nrhs), F32),
            v((width, width), F32),
            v((top, width, width), F32),
            v((width, width), BF16),
            v((width, width), BF16),
            v((top, width, width), BF16),
            v((top, width, width), BF16),
            v((nrhs, width), F32),
            v((2, chips, top, cols, width), F32),
            v((chips, top, cols, width), F32),
            v((2, chips, cols, width), F32),
            v((top - 1, cols, width), F32),
            v((EIGHT, chips, cols, width), F32),
            v((chips, cols, width), F32),
            v((chips, cols, width), F32),
            v((cols, width), F32),
            v((top, cols, width), F32),
            v((nb, chips, 2, share, width), F32),
            v((nr, chips, 2, share, nrhs), F32),
            v((nr, 2, chips, cols, width), F32),
            v((nb, width, width), BF16),
            v((nb, width, width), BF16),
            v((top - 1, 4, cols, width), F32),
            v((high, plan.groups, cols, width), F32),
            v((high, cols, width), F32),
            v((max(3, len(plan.nodes)), cols, width), F32),
            v((top, cols, width), F32),
            v((cols, width), F32),
            v((len(plan.nodes), cols, width), F32),
            v((top, 2, chips, cols, width), F32),
            v((nrhs, width), F32),
            v((width, nrhs), F32),
            dma((top + 2,)),
            dma((nb,)),
            dma((nr,)),
            dma((top + 1,)),
            dma((2, steps, nb)),
            dma((nb,)),
            dma((2, steps, nr)),
            dma((nr,)),
            dma((nb,)),
            dma((nb,)),
            dma((nr,)),
            dma((nr,)),
            dma((nb,)),
            dma((nb,)),
            dma((3,)),
            dma((3,)),
            dma((top,)),
            dma,
            dma((2,)),
            dma((2,)),
            dma,
            dma((top,)),
            dma,
            dma,
            dma((top,)),
            dma,
            dma((top - 1,)),
            dma((top - 1,)),
            dma((high,)),
            dma((high,)),
            dma((len(plan.nodes), plan.groups)),
            dma((top,)),
            dma((top,)),
            dma((top,)),
            dma((top,)),
            dma,
            dma((top,)),
            dma((top,)),
        ],
        compiler_params=pltpu.CompilerParams(
            collective_id=0, has_side_effects=True, vmem_limit_bytes=60 * 2**20
        ),
    )
    leaf, inner = call(
        leaf_rhs[0, 0], leaf_inv[0, 0], leaf_panel[0, 0], leaf_mask[0, 0],
        inner_rhs[0], inner_inv[0], inner_panel[0],
    )
    return leaf[None, None], inner[None]


def solution(mesh):
    in_specs = (
        P("row", "grp", None, None),
        P("row", "grp", None, None),
        P("row", "grp", None, None, None),
        P("row", "grp", None),
        P("row", "grp", None),
        P("row", "grp", None),
        P("row", None, "grp", None),
    )
    out_specs = (P("row", "grp", None, None), P("row", "grp", None))
    return jax.shard_map(
        per_device, mesh=mesh, in_specs=in_specs, out_specs=out_specs, check_vma=False
    )
```

```python
import functools

import jax
import jax.numpy as jnp
from jax import lax
from jax.experimental import pallas as pl
from jax.experimental.pallas import tpu as pltpu
from jax.sharding import PartitionSpec as P

F32 = jnp.float32
BF16 = jnp.bfloat16
NN = (((1,), (0,)), ((), ()))
NT = (((1,), (1,)), ((), ()))
EIGHT = 8


def split(x):
    high = x.astype(BF16)
    return high, (x - high.astype(F32)).astype(BF16)


def dot(a, b, dims):
    return lax.dot_general(a, b, dims, preferred_element_type=F32)


def product(a, b, dims=NN):
    return dot(a[0], b[0], dims) + (dot(a[0], b[1], dims) + dot(a[1], b[0], dims))


def thin(x, w, dims):
    rows = x.shape[0]
    high = x.astype(BF16).astype(F32)
    both = jnp.concatenate([high, x - high], axis=0).astype(BF16)
    first, second = dot(both, w[0], dims), dot(both, w[1], dims)
    return first[:rows] + (first[rows:] + second[:rows])


class Plan:
    def __init__(self, top, count):
        self.groups = count // EIGHT
        self.host3 = 12 if count > EIGHT else 4
        order = [(key, l) for key in (2, 6) for l in [0] + list(range(3, top + 1))]
        order += [(4, l) for l in [0] + list(range(4, top + 1))]
        self.mid = {key: i for i, key in enumerate(order)}
        self.mid_rhs = {2: 0, 6: 1, 4: 2}
        self.items = [(0, 2, 0, 4), (7, 2, 4, 4)]
        for place, l in zip((6, 1, 5, 3), range(3, top + 1)):
            self.items.append((place, l, 0, EIGHT))
        self.nodes = []
        for l in range(4, top):
            self.nodes += [(l, a) for a in range(2 ** (l - 1), count, 2**l)]
        self.nodes.append((top, 0))
        self.covers = {}
        for l, a in self.nodes:
            first = 0 if l == top else a - 2 ** (l - 1)
            last = count if l == top else a + 2 ** (l - 1)
            self.covers[a] = (first // EIGHT, last // EIGHT)
        self.below = {
            a: [d for k, d in self.nodes if k < l
                and self.covers[a][0] <= self.covers[d][0] < self.covers[a][1]]
            for l, a in self.nodes
        }
        order = []
        for l, a in self.nodes:
            order += [(d, l) for d in self.below[a]] + [(a, 0)]
        self.blocks = len(self.mid) + len(order)
        self.high = {key: len(self.mid) + i for i, key in enumerate(order)}
        self.rhs = 3 + len(self.nodes)
        self.high_rhs = {a: 3 + i for i, (l, a) in enumerate(self.nodes)}


def kernel(
    chips, count, plan,
    rhs_h, inv_h, pan_h, mask_s, irhs_h, iinv_h, ipan_h,
    leaf_out, inner_out,
    v_rhs, v_inv, v_pan, i_hi, i_lo, p_hi, p_lo, leaf_t,
    terms, terms_in, pieces1, upd,
    gather, gsum, gchips, gout, tin,
    blocks, rblock, rhs_t, b_hi, b_lo,
    vin, win, wout, fwd, sol, solb, xhigh, full, leaf_acc, turned,
    in_sem, arr_sem, arr_rhs, put_send,
    ring_recv, ring_send, rring_recv, rring_send, sib_recv, sib_send, rsib_recv, rsib_send,
    fw_recv, fw_send, rfw_recv, rfw_send,
    t_recv, t_send, a1_recv, a1_send,
    g_recv, g_send, gz_recv, gz_send, tin_recv, tin_send,
    v_recv, v_send, w_recv, w_send, x_send, down_recv, down_send,
    ag_recv, ag_send, left_send, pair_recv, pair_send,
):
    top = pan_h.shape[0]
    width, nrhs = v_rhs.shape
    member = lax.axis_index("grp")
    j = lax.axis_index("row")
    z, c = lax.div(member, 2), lax.rem(member, 2)
    other = 1 - c
    parity = lax.rem(j, 2)
    place = lax.rem(j, EIGHT)
    group = lax.div(j, EIGHT)
    start = j - place
    host2 = start + 2
    odd, even = parity == 1, parity == 0
    is2 = place == 2
    is3 = j == plan.host3
    mate = jnp.where(odd, j - 1, j + 1)
    lev = jnp.int32(1)
    for bit in range(1, top):
        lev = lev + (lax.rem(j, 2**bit) == 0).astype(jnp.int32)
    is0, is6 = place == 0, place == 6
    helps = jnp.logical_or(is0, is6)
    near = jnp.logical_not(jnp.logical_or(is0, place == 4))
    low = jnp.where(is6, top - 1, jnp.where(is0, 2 * (top - 1), 0))
    size = jnp.where(odd, top, jnp.where(is0, top - 2, top - 1))
    size = jnp.where(place == 4, 0, size)
    rlow = jnp.where(is6, 1, jnp.where(is0, 2, 0))
    rsize = jnp.where(place == 4, 0, 1)
    nmid = len(plan.mid)

    def at(zz=None, cc=None, jj=None):
        zz = z if zz is None else zz
        cc = c if cc is None else cc
        return {"grp": zz * 2 + cc, "row": j if jj is None else jj}

    def turn(step):
        return lax.rem(z + step + chips, chips)

    def remote(src, dst, send, recv, where):
        return pltpu.make_async_remote_copy(
            src_ref=src, dst_ref=dst, send_sem=send, recv_sem=recv,
            device_id=where, device_id_type=pl.DeviceIdType.MESH,
        )

    def local(src, dst, sem):
        return pltpu.make_async_copy(src, dst, sem)

    def await_bytes(ref, sem):
        pltpu.make_async_copy(ref, ref, sem).wait()

    rhs_in = local(rhs_h, v_rhs, in_sem.at[top])
    inv_in = local(inv_h, v_inv, in_sem.at[top + 1])
    rhs_in.start()
    inv_in.start()

    def panel_in(step):
        return local(pan_h.at[step], v_pan.at[step], in_sem.at[step])

    panel_in(0).start()

    def keep(l, slot):
        src = iinv_h if l == 0 else ipan_h.at[l - 1]
        local(src, blocks.at[slot, z, c], arr_sem.at[slot]).start()

    @pl.when(odd)
    def _():
        for l in [0] + list(range(2, top + 1)):
            keep(l, max(l - 1, 0))

    for key in (2, 6):
        @pl.when(place == key)
        def _(key=key):
            for l in [0] + list(range(3, top + 1)):
                keep(l, plan.mid[key, l])

    @pl.when(near)
    def _():
        local(irhs_h, rblock.at[rlow, z, c], arr_rhs.at[rlow]).start()

    for step in range(1, top):
        panel_in(step).start()

    barrier = pltpu.get_barrier_semaphore()

    def greet(where):
        pl.semaphore_signal(barrier, inc=1, device_id=where, device_id_type=pl.DeviceIdType.MESH)

    greet(at(cc=other))
    for step in range(1, chips):
        greet(at(zz=turn(step)))
    for step in range(chips):
        greet(at(zz=turn(step), jj=mate))

    for step in range(1, EIGHT):
        greet(at(jj=start + lax.rem(place + step, EIGHT)))

    @pl.when(is2)
    def _():
        greet(at(jj=plan.host3))

    @pl.when(is3)
    def _():
        for g in range(plan.groups):
            greet(at(jj=g * EIGHT + 2))
        for l, a in plan.nodes:
            greet(at(jj=a))

    @pl.when(is0)
    def _():
        greet(at(jj=plan.host3))

    expected = 2 * chips + EIGHT - 1 + jnp.where(is2, 1, 0) + jnp.where(is0, 1, 0)
    expected = expected + jnp.where(is3, plan.groups + len(plan.nodes), 0)

    def puts(slots, rhs_slots, key, levels, target):
        for n, l in enumerate([0] + levels):
            src = iinv_h if l == 0 else ipan_h.at[l - 1]
            slot = slots[key, l]
            yield remote(
                src, blocks.at[slot, z, c], put_send.at[n], arr_sem.at[slot], at(jj=target)
            )
        slot = rhs_slots[key]
        yield remote(
            irhs_h, rblock.at[slot, z, c], put_send.at[top], arr_rhs.at[slot], at(jj=target)
        )

    def each_put(act):
        @pl.when(place == 4)
        def _():
            for copy in puts(plan.mid, plan.mid_rhs, 4, list(range(4, top + 1)), start):
                act(copy)
        for l, a in plan.nodes:
            @pl.when(j == a)
            def _(l=l, a=a):
                levels = list(range(l + 1, top + 1))
                for copy in puts(plan.high, plan.high_rhs, a, levels, plan.host3):
                    act(copy)

    right, left = chips // 2, chips - 1 - chips // 2

    def heading(way, b):
        return (1 if way == 0 else -1) * (1 - 2 * lax.rem(b, 2))

    def ring(kind, way, step, b):
        ref = kind[0].at[b, turn(-step * heading(way, b)), c]
        return remote(
            ref, ref, kind[2].at[b], kind[3].at[way, step, b], at(zz=turn(heading(way, b)))
        )

    def ring_arrived(kind, way, step, b):
        src = turn(-(step + 1) * heading(way, b))
        await_bytes(kind[0].at[b, src, c], kind[3].at[way, step, b])
        pass_on(kind, b, src)

    kinds = (
        (blocks, arr_sem, ring_send, ring_recv, sib_send, sib_recv, fw_send, fw_recv),
        (rblock, arr_rhs, rring_send, rring_recv, rsib_send, rsib_recv, rfw_send, rfw_recv),
    )
    ranges = ((low, low + size), (rlow, rlow + rsize))
    ranges3 = (
        (nmid, jnp.where(is3, plan.blocks, nmid)),
        (3, jnp.where(is3, plan.rhs, 3)),
    )

    def pass_on(kind, b, src):
        @pl.when(passes(kind, b))
        def _():
            ref = kind[0].at[b, src, c]
            remote(ref, ref, kind[6].at[b], kind[7].at[b], at(jj=host2)).start()

    def first_step(ranges):
        for kind, (first, last) in zip(kinds, ranges):
            @pl.loop(first, last)
            def _(b):
                await_bytes(kind[0].at[b, z, c], kind[1].at[b])
                if right:
                    ring(kind, 0, 0, b).start()
                if left:
                    ring(kind, 1, 0, b).start()
                pass_on(kind, b, z)

    final = max(right, left)

    def next_step(step, ranges):
        for kind, (first, last) in zip(kinds, ranges):
            @pl.loop(first, last)
            def _(b):
                if step <= right:
                    ring_arrived(kind, 0, step - 1, b)
                    if step < right:
                        ring(kind, 0, step, b).start()
                if step <= left:
                    ring_arrived(kind, 1, step - 1, b)
                    if step < left:
                        ring(kind, 1, step, b).start()
                if step == final:
                    @pl.when(jnp.logical_not(passes(kind, b)))
                    def _():
                        share(kind, b).start()

    def passes(kind, b):
        return jnp.logical_and(helps, b < (nmid if kind[0] is blocks else 3))

    def share(kind, b):
        ref = kind[0].at[b, :, c]
        return remote(ref, ref, kind[4].at[b], kind[5].at[b], at(cc=other))

    def helped(kind, first, last):
        @pl.loop(first, last)
        def _(b):
            await_bytes(kind[0].at[b, :, c], kind[7].at[b])
            share(kind, b).start()

    def take_rhs(b):
        await_bytes(rblock.at[b, :, other], rsib_recv.at[b])
        rhs_t[b] = rblock[b].reshape(width, nrhs).T.reshape(rhs_t.shape[1:])

    def take_block(b):
        await_bytes(blocks.at[b, :, other], sib_recv.at[b])
        hi, lo = split(blocks[b].reshape(width, width))
        b_hi[b] = hi
        b_lo[b] = lo

    def block(b):
        return b_hi[b], b_lo[b]

    rhs_in.wait()
    inv_in.wait()
    hi, lo = split(v_inv[...])
    i_hi[...] = hi
    i_lo[...] = lo
    forward = product((hi, lo), split(v_rhs[...])).T
    leaf_t[...] = forward
    forward = split(forward)

    def swap_cores(l):
        return remote(
            terms.at[other, :, l], terms_in.at[:, l], t_send, t_recv.at[l], at(cc=other)
        )

    @pl.loop(0, top)
    def _(l):
        panel_in(l).wait()
        hi, lo = split(v_pan[l])
        p_hi[l] = hi
        p_lo[l] = lo
        term = product(forward, (hi, lo)) * mask_s[l].astype(F32)
        terms[:, :, l] = term.reshape(2, chips, -1, width)

    pl.semaphore_wait(barrier, expected)

    for l in range(top):
        swap_cores(l).start()
    each_put(lambda copy: copy.start())
    nowhere = lambda pair: (pair[0], jnp.where(near, pair[1], pair[0]))
    first_step([nowhere(pair) for pair in ranges])

    def add_cores(l):
        await_bytes(terms_in.at[:, l], t_recv.at[l])
        terms[c, :, l] = terms[c, :, l] + terms_in[:, l]

    def send_first(step):
        return remote(
            terms.at[c, turn(step), 0], pieces1.at[parity, z],
            a1_send.at[0 if step else 1], a1_recv.at[parity], at(zz=turn(step), jj=jnp.where(odd, j, mate)),
        )

    add_cores(0)

    @pl.when(even)
    def _():
        send_first(0).start()

    for step in range(1, chips):
        send_first(step).start()

    def collect(i):
        at_place, l, first, n = plan.items[i]
        return remote(
            terms.at[c, :, l - 1], gather.at[place], g_send.at[i], g_recv, at(jj=start + at_place)
        )

    def each_collect(l, act):
        for i, (at_place, level, first, n) in enumerate(plan.items):
            if level == l:
                @pl.when(jnp.logical_and(
                    place != at_place, jnp.logical_and(place >= first, place < first + n)
                ))
                def _(i=i):
                    act(collect(i))

    for l in range(2, top + 1):
        add_cores(l - 1)
        each_collect(l, lambda copy: copy.start())

    holds, my_item, my_level = place < 0, jnp.int32(0), jnp.int32(0)
    for i, (at_place, l, first, n) in enumerate(plan.items):
        mine = place == at_place
        holds = jnp.logical_or(holds, mine)
        my_item = jnp.where(mine, i, my_item)
        my_level = jnp.where(mine, l - 1, my_level)
    sources = jnp.where(my_item < 2, 4, EIGHT)
    origin = jnp.where(my_item == 1, 4, 0)

    def to_chip(step):
        return remote(gsum.at[turn(step)], gchips.at[z], gz_send, gz_recv, at(zz=turn(step)))

    def to_host():
        return remote(gout, tin.at[my_item], tin_send, tin_recv.at[my_item], at(jj=host2))

    def sum_places():
        @pl.when(holds)
        def _():
            @pl.when(my_item < 2)
            def _():
                await_bytes(gather.at[0:3], g_recv)

            @pl.when(my_item >= 2)
            def _():
                await_bytes(gather.at[0 : EIGHT - 1], g_recv)

            gsum[...] = terms[c, :, my_level]

            @pl.loop(1, sources)
            def _(k):
                r = origin + lax.rem(place - origin + k, sources)
                gsum[...] = gsum[...] + gather[r]

            for step in range(1, chips):
                to_chip(step).start()

    def sum_chips():
        @pl.when(holds)
        def _():
            await_bytes(gchips.at[0 : chips - 1], gz_recv)
            total = gsum[z]
            for step in range(1, chips):
                total = total + gchips[turn(step)]
            gout[...] = total
            to_host().start()

    far = lambda pair: (pair[0], jnp.where(near, pair[0], pair[1]))
    first_step([far(pair) for pair in ranges])
    first_step(ranges3)
    between = (final + 1) // 2
    for step in range(1, final + 1):
        next_step(step, ranges)
        next_step(step, ranges3)
        if step == between:
            sum_places()
    sum_chips()

    def send_v(l):
        return remote(
            upd.at[l - 2], vin.at[l - 2, lax.div(place, 2)], v_send.at[l - 2], v_recv.at[l - 2],
            at(jj=host2),
        )

    @pl.when(odd)
    def _():
        take_rhs(0)
        take_block(0)
        await_bytes(pieces1.at[0], a1_recv.at[0])
        await_bytes(pieces1.at[0, 0 : chips - 1], a1_recv.at[1])
        total = terms[c, z, 0] + pieces1[0, z]
        for step in range(1, chips):
            total = total + (pieces1[0, turn(step)] + pieces1[1, turn(step)])
        fwd[0] = thin(rhs_t[0, c, z] - total, block(0), NT)
        @pl.loop(2, top + 1)
        def _(l):
            take_block(l - 1)
            upd[l - 2] = thin(fwd[0], block(l - 1), NN)
            send_v(l).start()

    mid = plan.mid
    order = (1, 3, 5, 7, 0, 4, 6)

    def send_w(l):
        return remote(
            wout.at[l - 4], win.at[l - 4, group], w_send.at[l - 4], w_recv.at[l - 4],
            at(jj=plan.host3),
        )

    def arrived(l):
        await_bytes(vin.at[l - 2], v_recv.at[l - 2])
        for i, item in enumerate(plan.items):
            if item[1] == l:
                await_bytes(tin.at[i], tin_recv.at[i])

    def slots(l, first, last):
        total = tin[l - 1 if l > 2 else first // 2]
        for r in range(first, last):
            total = total + vin[l - 2, r]
        return total

    @pl.when(is2)
    def _():
        helped(kinds[1], 1, 3)
        helped(kinds[0], top - 1, nmid)
        for b in range(3):
            take_rhs(b)
        pl.loop(0, nmid)(take_block)
        arrived(2)
        fwd[0] = thin(rhs_t[0, c, z] - slots(2, 0, 2), block(mid[2, 0]), NT)
        fwd[1] = thin(rhs_t[1, c, z] - slots(2, 2, 4), block(mid[6, 0]), NT)
        arrived(3)
        fwd[2] = thin(
            rhs_t[2, c, z] - slots(3, 0, 4) - thin(fwd[0], block(mid[2, 3]), NN)
            - thin(fwd[1], block(mid[6, 3]), NN),
            block(mid[4, 0]), NT,
        )
        for l in range(4, top + 1):
            arrived(l)
            wout[l - 4] = slots(l, 0, 4) + (
                thin(fwd[0], block(mid[2, l]), NN) + thin(fwd[1], block(mid[6, l]), NN)
            ) + thin(fwd[2], block(mid[4, l]), NN)
            send_w(l).start()

    level_of = {a: l for l, a in plan.nodes}

    def send_x(a, g):
        n = plan.high_rhs[a] - 3
        l = level_of[a]
        return remote(
            xhigh.at[n], sol.at[l - 1], x_send.at[n, g], down_recv.at[l - 1],
            at(jj=g * EIGHT + 2),
        )

    @pl.when(is3)
    def _():
        for b in range(3, plan.rhs):
            take_rhs(b)
        pl.loop(nmid, plan.blocks)(take_block)
        for n, (l, a) in enumerate(plan.nodes):
            if n == 0 or plan.nodes[n - 1][0] != l:
                await_bytes(win.at[l - 4], w_recv.at[l - 4])
            total = rhs_t[3 + n, c, z]
            for g in range(*plan.covers[a]):
                total = total - win[l - 4, g]
            for d in plan.below[a]:
                total = total - thin(fwd[plan.high_rhs[d] - 3], block(plan.high[d, l]), NN)
            fwd[n] = thin(total, block(plan.high[a, 0]), NT)
        for l, a in reversed(plan.nodes):
            n = plan.high_rhs[a] - 3
            rest = fwd[n]
            for k, up in plan.nodes:
                if a in plan.below[up]:
                    rest = rest - thin(xhigh[plan.high_rhs[up] - 3], block(plan.high[a, k]), NT)
            xhigh[n] = thin(rest, block(plan.high[a, 0]), NN)
            for g in range(*plan.covers[a]):
                send_x(a, g).start()

    leaf_acc[...] = jnp.zeros_like(leaf_acc)

    def send_down(l, r, src=None):
        src = sol.at[l - 1] if src is None else src
        return remote(
            src, sol.at[l - 1], down_send.at[l - 1], down_recv.at[l - 1], at(jj=start + r)
        )

    def spread(l):
        full[l - 1, c, z] = sol[l - 1]
        for step in range(1, chips):
            remote(
                sol.at[l - 1], full.at[l - 1, c, z], ag_send.at[l - 1], ag_recv.at[l - 1],
                at(zz=turn(step)),
            ).start()

    def spread_left(step):
        return remote(
            sol.at[0], full.at[0, c, z], left_send, ag_recv.at[0], at(zz=turn(step), jj=mate)
        )

    @pl.when(is2)
    def _():
        rest = [fwd[0], fwd[1], fwd[2]]
        for l in range(top, 3, -1):
            await_bytes(sol.at[l - 1], down_recv.at[l - 1])
            for r in order:
                send_down(l, r).start()
            for n, key in enumerate((2, 6, 4)):
                rest[n] = rest[n] - thin(sol[l - 1], block(mid[key, l]), NT)
        sol[2] = thin(rest[2], block(mid[4, 0]), NN)
        for r in order:
            send_down(3, r).start()
        for n, key in enumerate((2, 6)):
            rest[n] = rest[n] - thin(sol[2], block(mid[key, 3]), NT)
        sol[1] = thin(rest[0], block(mid[2, 0]), NN)
        solb[...] = thin(rest[1], block(mid[6, 0]), NN)
        for r in order:
            send_down(2, r, None if r < 4 else solb).start()
        for l in range(top, 1, -1):
            spread(l)

    @pl.when(odd)
    def _():
        rest = fwd[0]
        for l in range(top, 1, -1):
            await_bytes(sol.at[l - 1], down_recv.at[l - 1])
            rest = rest - thin(sol[l - 1], block(l - 1), NT)
            if l > 3:
                spread(l)
        sol[0] = thin(rest, block(0), NN)
        spread(1)
        for step in range(chips):
            spread_left(step).start()
        for l in (3, 2):
            spread(l)

    @pl.when(jnp.logical_and(even, jnp.logical_not(is2)))
    def _():
        for l in range(top, 1, -1):
            await_bytes(sol.at[l - 1], down_recv.at[l - 1])
            spread(l)

    def pair(l):
        return remote(full.at[l, c], full.at[l, c], pair_send.at[l], pair_recv.at[l], at(cc=other))

    def leaf_back(l):
        await_bytes(full.at[l, other], pair_recv.at[l])
        ancestor = split(full[l].reshape(nrhs, width))
        leaf_acc[...] = leaf_acc[...] + mask_s[l].astype(F32) * product(
            ancestor, (p_hi[l], p_lo[l]), NT
        )

    @pl.loop(0, top)
    def _(i):
        l = top - 1 - i

        @pl.when(jnp.logical_and(l == 0, even))
        def _():
            await_bytes(full.at[0, c], ag_recv.at[0])

        @pl.when(jnp.logical_or(l > 0, odd))
        def _():
            await_bytes(full.at[l, c, 0 : chips - 1], ag_recv.at[l])

        pair(l).start()

        @pl.when(i >= 1)
        def _():
            leaf_back(l + 1)

    leaf_back(0)
    rest = split(leaf_t[...] - leaf_acc[...])
    leaf_out[...] = product(rest, (i_hi[...], i_lo[...])).T
    share_rows = inner_out.shape[0]
    turned[...] = full[lev - 1].reshape(nrhs, width).T
    inner_out[...] = turned[pl.ds(pl.multiple_of(member * share_rows, share_rows), share_rows), :]

    each_put(lambda copy: copy.wait_send())
    for some in (ranges, ranges3):
        for kind, (first, last) in zip(kinds, some):
            @pl.loop(first, last)
            def _(b):
                await_bytes(kind[0].at[b, 0 : chips - 1, 0], kind[2].at[b])
                gone = jnp.where(passes(kind, b), 1, 0)

                @pl.when(gone == 1)
                def _():
                    await_bytes(kind[0].at[b, :, c], kind[6].at[b])

                @pl.when(gone == 0)
                def _():
                    await_bytes(kind[0].at[b, :, c], kind[4].at[b])

    @pl.when(is2)
    def _():
        for kind, (first, last) in zip(kinds, ((top - 1, nmid), (1, 3))):
            @pl.loop(first, last)
            def _(b):
                await_bytes(kind[0].at[b, :, c], kind[4].at[b])
    await_bytes(terms.at[0], t_send)
    await_bytes(pieces1.at[0, 0 : chips - 1], a1_send.at[0])
    for l in range(2, top + 1):
        each_collect(l, lambda copy: copy.wait_send())

    @pl.when(holds)
    def _():
        await_bytes(gchips.at[0 : chips - 1], gz_send)
        to_host().wait_send()

    @pl.when(odd)
    def _():
        for l in range(2, top + 1):
            send_v(l).wait_send()

    @pl.when(is2)
    def _():
        for l in range(4, top + 1):
            send_w(l).wait_send()
        for l in range(2, top + 1):
            await_bytes(gather.at[0 : EIGHT - 1, 0], down_send.at[l - 1])

    @pl.when(is3)
    def _():
        for l, a in plan.nodes:
            for g in range(*plan.covers[a]):
                send_x(a, g).wait_send()

    @pl.loop(1, top)
    def _(l):
        await_bytes(full.at[l, 0, 0 : chips - 1], ag_send.at[l])

    @pl.when(odd)
    def _():
        await_bytes(full.at[0, 0, 0 : chips - 1], ag_send.at[0])
        await_bytes(full.at[0, 0], left_send)

    @pl.when(even)
    def _():
        send_first(0).wait_send()

    @pl.loop(0, top)
    def _(l):
        pair(l).wait_send()


def per_device(leaf_rhs, leaf_inv, leaf_panel, leaf_mask, inner_rhs, inner_inv, inner_panel):
    members, count = lax.axis_size("grp"), lax.axis_size("row")
    chips = members // 2
    width, nrhs = leaf_rhs.shape[2:]
    top = leaf_panel.shape[2]
    share, cols = width // members, nrhs // members
    plan = Plan(top, count)
    nb, nr, high = plan.blocks, plan.rhs, top - 3
    hbm = pl.BlockSpec(memory_space=pl.ANY)
    dma = pltpu.SemaphoreType.DMA
    steps = max(chips // 2, 1)
    v = pltpu.VMEM
    call = pl.pallas_call(
        functools.partial(kernel, chips, count, plan),
        out_shape=(
            pltpu.VMEM((width, nrhs), F32),
            pltpu.VMEM((share, nrhs), F32),
        ),
        in_specs=[hbm, hbm, hbm, pl.BlockSpec(memory_space=pltpu.SMEM), hbm, hbm, hbm],
        out_specs=[pl.BlockSpec(memory_space=pltpu.VMEM)] * 2,
        scratch_shapes=[
            v((width, nrhs), F32),
            v((width, width), F32),
            v((top, width, width), F32),
            v((width, width), BF16),
            v((width, width), BF16),
            v((top, width, width), BF16),
            v((top, width, width), BF16),
            v((nrhs, width), F32),
            v((2, chips, top, cols, width), F32),
            v((chips, top, cols, width), F32),
            v((2, chips, cols, width), F32),
            v((top - 1, cols, width), F32),
            v((EIGHT, chips, cols, width), F32),
            v((chips, cols, width), F32),
            v((chips, cols, width), F32),
            v((cols, width), F32),
            v((top, cols, width), F32),
            v((nb, chips, 2, share, width), F32),
            v((nr, chips, 2, share, nrhs), F32),
            v((nr, 2, chips, cols, width), F32),
            v((nb, width, width), BF16),
            v((nb, width, width), BF16),
            v((top - 1, 4, cols, width), F32),
            v((high, plan.groups, cols, width), F32),
            v((high, cols, width), F32),
            v((max(3, len(plan.nodes)), cols, width), F32),
            v((top, cols, width), F32),
            v((cols, width), F32),
            v((len(plan.nodes), cols, width), F32),
            v((top, 2, chips, cols, width), F32),
            v((nrhs, width), F32),
            v((width, nrhs), F32),
            dma((top + 2,)),
            dma((nb,)),
            dma((nr,)),
            dma((top + 1,)),
            dma((2, steps, nb)),
            dma((nb,)),
            dma((2, steps, nr)),
            dma((nr,)),
            dma((nb,)),
            dma((nb,)),
            dma((nr,)),
            dma((nr,)),
            dma((nb,)),
            dma((nb,)),
            dma((3,)),
            dma((3,)),
            dma((top,)),
            dma,
            dma((2,)),
            dma((2,)),
            dma,
            dma((top,)),
            dma,
            dma,
            dma((top,)),
            dma,
            dma((top - 1,)),
            dma((top - 1,)),
            dma((high,)),
            dma((high,)),
            dma((len(plan.nodes), plan.groups)),
            dma((top,)),
            dma((top,)),
            dma((top,)),
            dma((top,)),
            dma,
            dma((top,)),
            dma((top,)),
        ],
        compiler_params=pltpu.CompilerParams(
            collective_id=0, has_side_effects=True, vmem_limit_bytes=60 * 2**20
        ),
    )
    leaf, inner = call(
        leaf_rhs[0, 0], leaf_inv[0, 0], leaf_panel[0, 0], leaf_mask[0, 0],
        inner_rhs[0], inner_inv[0], inner_panel[0],
    )
    return leaf[None, None], inner[None]


def solution(mesh):
    in_specs = (
        P("row", "grp", None, None),
        P("row", "grp", None, None),
        P("row", "grp", None, None, None),
        P("row", "grp", None),
        P("row", "grp", None),
        P("row", "grp", None),
        P("row", None, "grp", None),
    )
    out_specs = (P("row", "grp", None, None), P("row", "grp", None))
    return jax.shard_map(
        per_device, mesh=mesh, in_specs=in_specs, out_specs=out_specs, check_vma=False
    )
```

```python
import functools

import jax
import jax.numpy as jnp
from jax import lax
from jax.experimental import pallas as pl
from jax.experimental.pallas import tpu as pltpu
from jax.sharding import PartitionSpec as P

F32 = jnp.float32
BF16 = jnp.bfloat16
NN = (((1,), (0,)), ((), ()))
NT = (((1,), (1,)), ((), ()))
EIGHT = 8


def split(x):
    high = x.astype(BF16)
    return high, (x - high.astype(F32)).astype(BF16)


def dot(a, b, dims):
    return lax.dot_general(a, b, dims, preferred_element_type=F32)


def product(a, b, dims=NN):
    return dot(a[0], b[0], dims) + (dot(a[0], b[1], dims) + dot(a[1], b[0], dims))


def thin(x, w, dims):
    rows = x.shape[0]
    high = x.astype(BF16).astype(F32)
    both = jnp.concatenate([high, x - high], axis=0).astype(BF16)
    first, second = dot(both, w[0], dims), dot(both, w[1], dims)
    return first[:rows] + (first[rows:] + second[:rows])


class Plan:
    def __init__(self, top, count):
        self.groups = count // EIGHT
        self.host3 = 12 if count > EIGHT else 4
        order = [(key, l) for key in (2, 6) for l in [0] + list(range(3, top + 1))]
        order += [(4, l) for l in [0] + list(range(4, top + 1))]
        self.mid = {key: i for i, key in enumerate(order)}
        self.mid_rhs = {2: 0, 6: 1, 4: 2}
        self.lent = 2
        self.items = [(0, 2, 0, 4), (7, 2, 4, 4)]
        for place, l in zip((6, 1, 5, 3), range(3, top + 1)):
            self.items.append((place, l, 0, EIGHT))
        self.nodes = []
        for l in range(4, top):
            self.nodes += [(l, a) for a in range(2 ** (l - 1), count, 2**l)]
        self.nodes.append((top, 0))
        self.covers = {}
        for l, a in self.nodes:
            first = 0 if l == top else a - 2 ** (l - 1)
            last = count if l == top else a + 2 ** (l - 1)
            self.covers[a] = (first // EIGHT, last // EIGHT)
        self.below = {
            a: [d for k, d in self.nodes if k < l
                and self.covers[a][0] <= self.covers[d][0] < self.covers[a][1]]
            for l, a in self.nodes
        }
        order = []
        for l, a in self.nodes:
            order += [(d, l) for d in self.below[a]] + [(a, 0)]
        self.blocks = len(self.mid) + len(order)
        self.high = {key: len(self.mid) + i for i, key in enumerate(order)}
        self.rhs = 3 + len(self.nodes)
        self.high_rhs = {a: 3 + i for i, (l, a) in enumerate(self.nodes)}


def kernel(
    chips, count, plan,
    rhs_h, inv_h, pan_h, mask_s, irhs_h, iinv_h, ipan_h,
    leaf_out, inner_out,
    v_rhs, v_inv, v_pan, i_hi, i_lo, p_hi, p_lo, leaf_t,
    terms, terms_in, pieces1, upd,
    gather, gsum, gchips, gout, tin,
    blocks, rblock, rhs_t, b_hi, b_lo,
    vin, win, wout, fwd, sol, solb, xhigh, full, leaf_acc, turned,
    in_sem, arr_sem, arr_rhs, put_send,
    ring_recv, ring_send, rring_recv, rring_send, sib_recv, sib_send, rsib_recv, rsib_send,
    fw_recv, fw_send, rfw_recv, rfw_send,
    t_recv, t_send, a1_recv, a1_send,
    g_recv, g_send, gz_recv, gz_send, tin_recv, tin_send,
    v_recv, v_send, w_recv, w_send, x_send, down_recv, down_send,
    ag_recv, ag_send, left_send, pair_recv, pair_send,
):
    top = pan_h.shape[0]
    width, nrhs = v_rhs.shape
    member = lax.axis_index("grp")
    j = lax.axis_index("row")
    z, c = lax.div(member, 2), lax.rem(member, 2)
    other = 1 - c
    parity = lax.rem(j, 2)
    place = lax.rem(j, EIGHT)
    group = lax.div(j, EIGHT)
    start = j - place
    host2 = start + 2
    odd, even = parity == 1, parity == 0
    is2 = place == 2
    is3 = j == plan.host3
    mate = jnp.where(odd, j - 1, j + 1)
    lev = jnp.int32(1)
    for bit in range(1, top):
        lev = lev + (lax.rem(j, 2**bit) == 0).astype(jnp.int32)
    is0, is6 = place == 0, place == 6
    helps = jnp.logical_or(is0, is6)
    near = jnp.logical_not(jnp.logical_or(is0, place == 4))
    lent = top - 1 + plan.lent
    low = jnp.where(is6, lent, jnp.where(is0, 2 * (top - 1), 0))
    size = jnp.where(odd, top, jnp.where(is0, top - 2, 2 * (top - 1) - lent))
    size = jnp.where(is2, lent, jnp.where(place == 4, 0, size))
    here = jnp.where(is0, 0, jnp.where(is2, top - 1, size))
    rlow = jnp.where(is6, 1, jnp.where(is0, 2, 0))
    rsize = jnp.where(place == 4, 0, 1)
    nmid = len(plan.mid)

    def at(zz=None, cc=None, jj=None):
        zz = z if zz is None else zz
        cc = c if cc is None else cc
        return {"grp": zz * 2 + cc, "row": j if jj is None else jj}

    def turn(step):
        return lax.rem(z + step + chips, chips)

    def remote(src, dst, send, recv, where):
        return pltpu.make_async_remote_copy(
            src_ref=src, dst_ref=dst, send_sem=send, recv_sem=recv,
            device_id=where, device_id_type=pl.DeviceIdType.MESH,
        )

    def local(src, dst, sem):
        return pltpu.make_async_copy(src, dst, sem)

    def await_bytes(ref, sem):
        pltpu.make_async_copy(ref, ref, sem).wait()

    rhs_in = local(rhs_h, v_rhs, in_sem.at[top])
    inv_in = local(inv_h, v_inv, in_sem.at[top + 1])
    rhs_in.start()
    inv_in.start()

    def panel_in(step):
        return local(pan_h.at[step], v_pan.at[step], in_sem.at[step])

    panel_in(0).start()

    def keep(l, slot):
        src = iinv_h if l == 0 else ipan_h.at[l - 1]
        local(src, blocks.at[slot, z, c], arr_sem.at[slot]).start()

    @pl.when(odd)
    def _():
        for l in [0] + list(range(2, top + 1)):
            keep(l, max(l - 1, 0))

    for key in (2, 6):
        @pl.when(place == key)
        def _(key=key):
            for l in ([0] + list(range(3, top + 1)))[0 if key == 2 else plan.lent :]:
                keep(l, plan.mid[key, l])

    @pl.when(near)
    def _():
        local(irhs_h, rblock.at[rlow, z, c], arr_rhs.at[rlow]).start()

    for step in range(1, top):
        panel_in(step).start()

    barrier = pltpu.get_barrier_semaphore()

    def greet(where):
        pl.semaphore_signal(barrier, inc=1, device_id=where, device_id_type=pl.DeviceIdType.MESH)

    greet(at(cc=other))
    for step in range(1, chips):
        greet(at(zz=turn(step)))
    for step in range(chips):
        greet(at(zz=turn(step), jj=mate))

    for step in range(1, EIGHT):
        greet(at(jj=start + lax.rem(place + step, EIGHT)))

    @pl.when(is2)
    def _():
        greet(at(jj=plan.host3))

    @pl.when(is3)
    def _():
        for g in range(plan.groups):
            greet(at(jj=g * EIGHT + 2))
        for l, a in plan.nodes:
            greet(at(jj=a))

    @pl.when(is0)
    def _():
        greet(at(jj=plan.host3))

    expected = 2 * chips + EIGHT - 1 + jnp.where(is2, 1, 0) + jnp.where(is0, 1, 0)
    expected = expected + jnp.where(is3, plan.groups + len(plan.nodes), 0)

    def puts(slots, rhs_slots, key, levels, target):
        for n, l in enumerate([0] + levels):
            src = iinv_h if l == 0 else ipan_h.at[l - 1]
            slot = slots[key, l]
            yield remote(
                src, blocks.at[slot, z, c], put_send.at[n], arr_sem.at[slot], at(jj=target)
            )
        slot = rhs_slots[key]
        yield remote(
            irhs_h, rblock.at[slot, z, c], put_send.at[top], arr_rhs.at[slot], at(jj=target)
        )

    def each_put(act):
        @pl.when(place == 6)
        def _():
            for n, l in enumerate(([0] + list(range(3, top + 1)))[: plan.lent]):
                src = iinv_h if l == 0 else ipan_h.at[l - 1]
                slot = plan.mid[6, l]
                act(remote(
                    src, blocks.at[slot, z, c], put_send.at[n], arr_sem.at[slot], at(jj=host2)
                ))

        @pl.when(place == 4)
        def _():
            for copy in puts(plan.mid, plan.mid_rhs, 4, list(range(4, top + 1)), start):
                act(copy)
        for l, a in plan.nodes:
            @pl.when(j == a)
            def _(l=l, a=a):
                levels = list(range(l + 1, top + 1))
                for copy in puts(plan.high, plan.high_rhs, a, levels, plan.host3):
                    act(copy)

    right, left = chips // 2, chips - 1 - chips // 2

    def heading(way, b):
        return (1 if way == 0 else -1) * (1 - 2 * lax.rem(b, 2))

    def ring(kind, way, step, b):
        ref = kind[0].at[b, turn(-step * heading(way, b)), c]
        return remote(
            ref, ref, kind[2].at[b], kind[3].at[way, step, b], at(zz=turn(heading(way, b)))
        )

    def ring_arrived(kind, way, step, b):
        src = turn(-(step + 1) * heading(way, b))
        await_bytes(kind[0].at[b, src, c], kind[3].at[way, step, b])
        pass_on(kind, b, src)

    kinds = (
        (blocks, arr_sem, ring_send, ring_recv, sib_send, sib_recv, fw_send, fw_recv),
        (rblock, arr_rhs, rring_send, rring_recv, rsib_send, rsib_recv, rfw_send, rfw_recv),
    )
    ranges = ((low, low + size), (rlow, rlow + rsize))
    ranges3 = (
        (nmid, jnp.where(is3, plan.blocks, nmid)),
        (3, jnp.where(is3, plan.rhs, 3)),
    )

    def pass_on(kind, b, src):
        @pl.when(passes(kind, b))
        def _():
            ref = kind[0].at[b, src, c]
            remote(ref, ref, kind[6].at[b], kind[7].at[b], at(jj=host2)).start()

    def first_step(ranges):
        for kind, (first, last) in zip(kinds, ranges):
            @pl.loop(first, last)
            def _(b):
                await_bytes(kind[0].at[b, z, c], kind[1].at[b])
                if right:
                    ring(kind, 0, 0, b).start()
                if left:
                    ring(kind, 1, 0, b).start()
                pass_on(kind, b, z)

    final = max(right, left)

    def next_step(step, ranges):
        for kind, (first, last) in zip(kinds, ranges):
            @pl.loop(first, last)
            def _(b):
                if step <= right:
                    ring_arrived(kind, 0, step - 1, b)
                    if step < right:
                        ring(kind, 0, step, b).start()
                if step <= left:
                    ring_arrived(kind, 1, step - 1, b)
                    if step < left:
                        ring(kind, 1, step, b).start()
                if step == final:
                    @pl.when(jnp.logical_not(passes(kind, b)))
                    def _():
                        share(kind, b).start()

    def passes(kind, b):
        return jnp.logical_and(helps, b < (nmid if kind[0] is blocks else 3))

    def share(kind, b):
        ref = kind[0].at[b, :, c]
        return remote(ref, ref, kind[4].at[b], kind[5].at[b], at(cc=other))

    def helped(kind, first, last):
        @pl.loop(first, last)
        def _(b):
            await_bytes(kind[0].at[b, :, c], kind[7].at[b])
            share(kind, b).start()

    def take_rhs(b):
        await_bytes(rblock.at[b, :, other], rsib_recv.at[b])
        rhs_t[b] = rblock[b].reshape(width, nrhs).T.reshape(rhs_t.shape[1:])

    def take_block(b):
        await_bytes(blocks.at[b, :, other], sib_recv.at[b])
        hi, lo = split(blocks[b].reshape(width, width))
        b_hi[b] = hi
        b_lo[b] = lo

    def block(b):
        return b_hi[b], b_lo[b]

    rhs_in.wait()
    inv_in.wait()
    hi, lo = split(v_inv[...])
    i_hi[...] = hi
    i_lo[...] = lo
    forward = product((hi, lo), split(v_rhs[...])).T
    leaf_t[...] = forward
    forward = split(forward)

    def swap_cores(l):
        return remote(
            terms.at[other, :, l], terms_in.at[:, l], t_send, t_recv.at[l], at(cc=other)
        )

    @pl.loop(0, top)
    def _(l):
        panel_in(l).wait()
        hi, lo = split(v_pan[l])
        p_hi[l] = hi
        p_lo[l] = lo
        term = product(forward, (hi, lo)) * mask_s[l].astype(F32)
        terms[:, :, l] = term.reshape(2, chips, -1, width)

    pl.semaphore_wait(barrier, expected)

    for l in range(top):
        swap_cores(l).start()
    each_put(lambda copy: copy.start())
    rhere = jnp.where(near, rsize, 0)
    first_step([(low, low + here), (rlow, rlow + rhere)])

    def add_cores(l):
        await_bytes(terms_in.at[:, l], t_recv.at[l])
        terms[c, :, l] = terms[c, :, l] + terms_in[:, l]

    def send_first(step):
        return remote(
            terms.at[c, turn(step), 0], pieces1.at[parity, z],
            a1_send.at[0 if step else 1], a1_recv.at[parity], at(zz=turn(step), jj=jnp.where(odd, j, mate)),
        )

    add_cores(0)

    @pl.when(even)
    def _():
        send_first(0).start()

    for step in range(1, chips):
        send_first(step).start()

    def collect(i):
        at_place, l, first, n = plan.items[i]
        return remote(
            terms.at[c, :, l - 1], gather.at[place], g_send.at[i], g_recv, at(jj=start + at_place)
        )

    def each_collect(l, act):
        for i, (at_place, level, first, n) in enumerate(plan.items):
            if level == l:
                @pl.when(jnp.logical_and(
                    place != at_place, jnp.logical_and(place >= first, place < first + n)
                ))
                def _(i=i):
                    act(collect(i))

    for l in range(2, top + 1):
        add_cores(l - 1)
        each_collect(l, lambda copy: copy.start())

    holds, my_item, my_level = place < 0, jnp.int32(0), jnp.int32(0)
    for i, (at_place, l, first, n) in enumerate(plan.items):
        mine = place == at_place
        holds = jnp.logical_or(holds, mine)
        my_item = jnp.where(mine, i, my_item)
        my_level = jnp.where(mine, l - 1, my_level)
    sources = jnp.where(my_item < 2, 4, EIGHT)
    origin = jnp.where(my_item == 1, 4, 0)

    def to_chip(step):
        return remote(gsum.at[turn(step)], gchips.at[z], gz_send, gz_recv, at(zz=turn(step)))

    def to_host():
        return remote(gout, tin.at[my_item], tin_send, tin_recv.at[my_item], at(jj=host2))

    def sum_places():
        @pl.when(holds)
        def _():
            @pl.when(my_item < 2)
            def _():
                await_bytes(gather.at[0:3], g_recv)

            @pl.when(my_item >= 2)
            def _():
                await_bytes(gather.at[0 : EIGHT - 1], g_recv)

            gsum[...] = terms[c, :, my_level]

            @pl.loop(1, sources)
            def _(k):
                r = origin + lax.rem(place - origin + k, sources)
                gsum[...] = gsum[...] + gather[r]

            for step in range(1, chips):
                to_chip(step).start()

    def sum_chips():
        @pl.when(holds)
        def _():
            await_bytes(gchips.at[0 : chips - 1], gz_recv)
            total = gsum[z]
            for step in range(1, chips):
                total = total + gchips[turn(step)]
            gout[...] = total
            to_host().start()

    first_step([(low + here, low + size), (rlow + rhere, rlow + rsize)])
    first_step(ranges3)
    between = (final + 1) // 2
    for step in range(1, final + 1):
        next_step(step, ranges)
        next_step(step, ranges3)
        if step == between:
            sum_places()
    sum_chips()

    def send_v(l):
        return remote(
            upd.at[l - 2], vin.at[l - 2, lax.div(place, 2)], v_send.at[l - 2], v_recv.at[l - 2],
            at(jj=host2),
        )

    @pl.when(odd)
    def _():
        take_rhs(0)
        take_block(0)
        await_bytes(pieces1.at[0], a1_recv.at[0])
        await_bytes(pieces1.at[0, 0 : chips - 1], a1_recv.at[1])
        total = terms[c, z, 0] + pieces1[0, z]
        for step in range(1, chips):
            total = total + (pieces1[0, turn(step)] + pieces1[1, turn(step)])
        fwd[0] = thin(rhs_t[0, c, z] - total, block(0), NT)
        @pl.loop(2, top + 1)
        def _(l):
            take_block(l - 1)
            upd[l - 2] = thin(fwd[0], block(l - 1), NN)
            send_v(l).start()

    mid = plan.mid
    order = (1, 3, 5, 7, 0, 4, 6)

    def send_w(l):
        return remote(
            wout.at[l - 4], win.at[l - 4, group], w_send.at[l - 4], w_recv.at[l - 4],
            at(jj=plan.host3),
        )

    def arrived(l):
        await_bytes(vin.at[l - 2], v_recv.at[l - 2])
        for i, item in enumerate(plan.items):
            if item[1] == l:
                await_bytes(tin.at[i], tin_recv.at[i])

    def slots(l, first, last):
        total = tin[l - 1 if l > 2 else first // 2]
        for r in range(first, last):
            total = total + vin[l - 2, r]
        return total

    @pl.when(is2)
    def _():
        helped(kinds[1], 1, 3)
        helped(kinds[0], lent, nmid)
        for b in range(3):
            take_rhs(b)
        pl.loop(0, nmid)(take_block)
        arrived(2)
        fwd[0] = thin(rhs_t[0, c, z] - slots(2, 0, 2), block(mid[2, 0]), NT)
        fwd[1] = thin(rhs_t[1, c, z] - slots(2, 2, 4), block(mid[6, 0]), NT)
        arrived(3)
        fwd[2] = thin(
            rhs_t[2, c, z] - slots(3, 0, 4) - thin(fwd[0], block(mid[2, 3]), NN)
            - thin(fwd[1], block(mid[6, 3]), NN),
            block(mid[4, 0]), NT,
        )
        for l in range(4, top + 1):
            arrived(l)
            wout[l - 4] = slots(l, 0, 4) + (
                thin(fwd[0], block(mid[2, l]), NN) + thin(fwd[1], block(mid[6, l]), NN)
            ) + thin(fwd[2], block(mid[4, l]), NN)
            send_w(l).start()

    level_of = {a: l for l, a in plan.nodes}

    def send_x(a, g):
        n = plan.high_rhs[a] - 3
        l = level_of[a]
        return remote(
            xhigh.at[n], sol.at[l - 1], x_send.at[n, g], down_recv.at[l - 1],
            at(jj=g * EIGHT + 2),
        )

    @pl.when(is3)
    def _():
        for b in range(3, plan.rhs):
            take_rhs(b)
        pl.loop(nmid, plan.blocks)(take_block)
        for n, (l, a) in enumerate(plan.nodes):
            if n == 0 or plan.nodes[n - 1][0] != l:
                await_bytes(win.at[l - 4], w_recv.at[l - 4])
            total = rhs_t[3 + n, c, z]
            for g in range(*plan.covers[a]):
                total = total - win[l - 4, g]
            for d in plan.below[a]:
                total = total - thin(fwd[plan.high_rhs[d] - 3], block(plan.high[d, l]), NN)
            fwd[n] = thin(total, block(plan.high[a, 0]), NT)
        for l, a in reversed(plan.nodes):
            n = plan.high_rhs[a] - 3
            rest = fwd[n]
            for k, up in plan.nodes:
                if a in plan.below[up]:
                    rest = rest - thin(xhigh[plan.high_rhs[up] - 3], block(plan.high[a, k]), NT)
            xhigh[n] = thin(rest, block(plan.high[a, 0]), NN)
            for g in range(*plan.covers[a]):
                send_x(a, g).start()

    leaf_acc[...] = jnp.zeros_like(leaf_acc)

    def send_down(l, r, src=None):
        src = sol.at[l - 1] if src is None else src
        return remote(
            src, sol.at[l - 1], down_send.at[l - 1], down_recv.at[l - 1], at(jj=start + r)
        )

    def spread(l):
        full[l - 1, c, z] = sol[l - 1]
        for step in range(1, chips):
            remote(
                sol.at[l - 1], full.at[l - 1, c, z], ag_send.at[l - 1], ag_recv.at[l - 1],
                at(zz=turn(step)),
            ).start()

    def spread_left(step):
        return remote(
            sol.at[0], full.at[0, c, z], left_send, ag_recv.at[0], at(zz=turn(step), jj=mate)
        )

    @pl.when(is2)
    def _():
        rest = [fwd[0], fwd[1], fwd[2]]
        for l in range(top, 3, -1):
            await_bytes(sol.at[l - 1], down_recv.at[l - 1])
            for r in order:
                send_down(l, r).start()
            for n, key in enumerate((2, 6, 4)):
                rest[n] = rest[n] - thin(sol[l - 1], block(mid[key, l]), NT)
            if l > 4:
                spread(l)
        sol[2] = thin(rest[2], block(mid[4, 0]), NN)
        for r in order:
            send_down(3, r).start()
        for n, key in enumerate((2, 6)):
            rest[n] = rest[n] - thin(sol[2], block(mid[key, 3]), NT)
        sol[1] = thin(rest[0], block(mid[2, 0]), NN)
        solb[...] = thin(rest[1], block(mid[6, 0]), NN)
        for r in order:
            send_down(2, r, None if r < 4 else solb).start()
        for l in range(min(top, 4), 1, -1):
            spread(l)

    @pl.when(odd)
    def _():
        rest = fwd[0]
        for l in range(top, 1, -1):
            await_bytes(sol.at[l - 1], down_recv.at[l - 1])
            rest = rest - thin(sol[l - 1], block(l - 1), NT)
            if l > 3:
                spread(l)
        sol[0] = thin(rest, block(0), NN)
        spread(1)
        for step in range(chips):
            spread_left(step).start()
        for l in (3, 2):
            spread(l)

    @pl.when(jnp.logical_and(even, jnp.logical_not(is2)))
    def _():
        for l in range(top, 1, -1):
            await_bytes(sol.at[l - 1], down_recv.at[l - 1])
            spread(l)

    def pair(l):
        return remote(full.at[l, c], full.at[l, c], pair_send.at[l], pair_recv.at[l], at(cc=other))

    def leaf_back(l):
        await_bytes(full.at[l, other], pair_recv.at[l])
        ancestor = split(full[l].reshape(nrhs, width))
        leaf_acc[...] = leaf_acc[...] + mask_s[l].astype(F32) * product(
            ancestor, (p_hi[l], p_lo[l]), NT
        )

    @pl.loop(0, top)
    def _(i):
        l = top - 1 - i

        @pl.when(jnp.logical_and(l == 0, even))
        def _():
            await_bytes(full.at[0, c], ag_recv.at[0])

        @pl.when(jnp.logical_or(l > 0, odd))
        def _():
            await_bytes(full.at[l, c, 0 : chips - 1], ag_recv.at[l])

        pair(l).start()

        @pl.when(i >= 1)
        def _():
            leaf_back(l + 1)

    leaf_back(0)
    rest = split(leaf_t[...] - leaf_acc[...])
    leaf_out[...] = product(rest, (i_hi[...], i_lo[...])).T
    share_rows = inner_out.shape[0]
    turned[...] = full[lev - 1].reshape(nrhs, width).T
    inner_out[...] = turned[pl.ds(pl.multiple_of(member * share_rows, share_rows), share_rows), :]

    each_put(lambda copy: copy.wait_send())
    for some in (ranges, ranges3):
        for kind, (first, last) in zip(kinds, some):
            @pl.loop(first, last)
            def _(b):
                await_bytes(kind[0].at[b, 0 : chips - 1, 0], kind[2].at[b])
                gone = jnp.where(passes(kind, b), 1, 0)

                @pl.when(gone == 1)
                def _():
                    await_bytes(kind[0].at[b, :, c], kind[6].at[b])

                @pl.when(gone == 0)
                def _():
                    await_bytes(kind[0].at[b, :, c], kind[4].at[b])

    @pl.when(is2)
    def _():
        for kind, (first, last) in zip(kinds, ((lent, nmid), (1, 3))):
            @pl.loop(first, last)
            def _(b):
                await_bytes(kind[0].at[b, :, c], kind[4].at[b])
    await_bytes(terms.at[0], t_send)
    await_bytes(pieces1.at[0, 0 : chips - 1], a1_send.at[0])
    for l in range(2, top + 1):
        each_collect(l, lambda copy: copy.wait_send())

    @pl.when(holds)
    def _():
        await_bytes(gchips.at[0 : chips - 1], gz_send)
        to_host().wait_send()

    @pl.when(odd)
    def _():
        for l in range(2, top + 1):
            send_v(l).wait_send()

    @pl.when(is2)
    def _():
        for l in range(4, top + 1):
            send_w(l).wait_send()
        for l in range(2, top + 1):
            await_bytes(gather.at[0 : EIGHT - 1, 0], down_send.at[l - 1])

    @pl.when(is3)
    def _():
        for l, a in plan.nodes:
            for g in range(*plan.covers[a]):
                send_x(a, g).wait_send()

    @pl.loop(1, top)
    def _(l):
        await_bytes(full.at[l, 0, 0 : chips - 1], ag_send.at[l])

    @pl.when(odd)
    def _():
        await_bytes(full.at[0, 0, 0 : chips - 1], ag_send.at[0])
        await_bytes(full.at[0, 0], left_send)

    @pl.when(even)
    def _():
        send_first(0).wait_send()

    @pl.loop(0, top)
    def _(l):
        pair(l).wait_send()


def per_device(leaf_rhs, leaf_inv, leaf_panel, leaf_mask, inner_rhs, inner_inv, inner_panel):
    members, count = lax.axis_size("grp"), lax.axis_size("row")
    chips = members // 2
    width, nrhs = leaf_rhs.shape[2:]
    top = leaf_panel.shape[2]
    share, cols = width // members, nrhs // members
    plan = Plan(top, count)
    nb, nr, high = plan.blocks, plan.rhs, top - 3
    hbm = pl.BlockSpec(memory_space=pl.ANY)
    dma = pltpu.SemaphoreType.DMA
    steps = max(chips // 2, 1)
    v = pltpu.VMEM
    call = pl.pallas_call(
        functools.partial(kernel, chips, count, plan),
        out_shape=(
            pltpu.VMEM((width, nrhs), F32),
            pltpu.VMEM((share, nrhs), F32),
        ),
        in_specs=[hbm, hbm, hbm, pl.BlockSpec(memory_space=pltpu.SMEM), hbm, hbm, hbm],
        out_specs=[pl.BlockSpec(memory_space=pltpu.VMEM)] * 2,
        scratch_shapes=[
            v((width, nrhs), F32),
            v((width, width), F32),
            v((top, width, width), F32),
            v((width, width), BF16),
            v((width, width), BF16),
            v((top, width, width), BF16),
            v((top, width, width), BF16),
            v((nrhs, width), F32),
            v((2, chips, top, cols, width), F32),
            v((chips, top, cols, width), F32),
            v((2, chips, cols, width), F32),
            v((top - 1, cols, width), F32),
            v((EIGHT, chips, cols, width), F32),
            v((chips, cols, width), F32),
            v((chips, cols, width), F32),
            v((cols, width), F32),
            v((top, cols, width), F32),
            v((nb, chips, 2, share, width), F32),
            v((nr, chips, 2, share, nrhs), F32),
            v((nr, 2, chips, cols, width), F32),
            v((nb, width, width), BF16),
            v((nb, width, width), BF16),
            v((top - 1, 4, cols, width), F32),
            v((high, plan.groups, cols, width), F32),
            v((high, cols, width), F32),
            v((max(3, len(plan.nodes)), cols, width), F32),
            v((top, cols, width), F32),
            v((cols, width), F32),
            v((len(plan.nodes), cols, width), F32),
            v((top, 2, chips, cols, width), F32),
            v((nrhs, width), F32),
            v((width, nrhs), F32),
            dma((top + 2,)),
            dma((nb,)),
            dma((nr,)),
            dma((top + 1,)),
            dma((2, steps, nb)),
            dma((nb,)),
            dma((2, steps, nr)),
            dma((nr,)),
            dma((nb,)),
            dma((nb,)),
            dma((nr,)),
            dma((nr,)),
            dma((nb,)),
            dma((nb,)),
            dma((3,)),
            dma((3,)),
            dma((top,)),
            dma,
            dma((2,)),
            dma((2,)),
            dma,
            dma((top,)),
            dma,
            dma,
            dma((top,)),
            dma,
            dma((top - 1,)),
            dma((top - 1,)),
            dma((high,)),
            dma((high,)),
            dma((len(plan.nodes), plan.groups)),
            dma((top,)),
            dma((top,)),
            dma((top,)),
            dma((top,)),
            dma,
            dma((top,)),
            dma((top,)),
        ],
        compiler_params=pltpu.CompilerParams(
            collective_id=0, has_side_effects=True, vmem_limit_bytes=60 * 2**20
        ),
    )
    leaf, inner = call(
        leaf_rhs[0, 0], leaf_inv[0, 0], leaf_panel[0, 0], leaf_mask[0, 0],
        inner_rhs[0], inner_inv[0], inner_panel[0],
    )
    return leaf[None, None], inner[None]


def solution(mesh):
    in_specs = (
        P("row", "grp", None, None),
        P("row", "grp", None, None),
        P("row", "grp", None, None, None),
        P("row", "grp", None),
        P("row", "grp", None),
        P("row", "grp", None),
        P("row", None, "grp", None),
    )
    out_specs = (P("row", "grp", None, None), P("row", "grp", None))
    return jax.shard_map(
        per_device, mesh=mesh, in_specs=in_specs, out_specs=out_specs, check_vma=False
    )
```

```python
import functools

import jax
import jax.numpy as jnp
from jax import lax
from jax.experimental import pallas as pl
from jax.experimental.pallas import tpu as pltpu
from jax.sharding import PartitionSpec as P

F32 = jnp.float32
BF16 = jnp.bfloat16
NN = (((1,), (0,)), ((), ()))
NT = (((1,), (1,)), ((), ()))
EIGHT = 8


def split(x):
    high = x.astype(BF16)
    return high, (x - high.astype(F32)).astype(BF16)


def dot(a, b, dims):
    return lax.dot_general(a, b, dims, preferred_element_type=F32)


def product(a, b, dims=NN):
    return dot(a[0], b[0], dims) + (dot(a[0], b[1], dims) + dot(a[1], b[0], dims))


def thin(x, w, dims):
    rows = x.shape[0]
    high = x.astype(BF16).astype(F32)
    both = jnp.concatenate([high, x - high], axis=0).astype(BF16)
    first, second = dot(both, w[0], dims), dot(both, w[1], dims)
    return first[:rows] + (first[rows:] + second[:rows])


class Plan:
    def __init__(self, top, count):
        self.groups = count // EIGHT
        self.host3 = 12 if count > EIGHT else 4
        order = [(key, l) for key in (2, 6) for l in [0] + list(range(3, top + 1))]
        order += [(4, l) for l in [0] + list(range(4, top + 1))]
        self.mid = {key: i for i, key in enumerate(order)}
        self.mid_rhs = {2: 0, 6: 1, 4: 2}
        self.items = [(0, 2, 0, 4), (7, 2, 4, 4)]
        for place, l in zip((6, 1, 5, 3), range(3, top + 1)):
            self.items.append((place, l, 0, EIGHT))
        self.nodes = []
        for l in range(4, top):
            self.nodes += [(l, a) for a in range(2 ** (l - 1), count, 2**l)]
        self.nodes.append((top, 0))
        self.covers = {}
        for l, a in self.nodes:
            first = 0 if l == top else a - 2 ** (l - 1)
            last = count if l == top else a + 2 ** (l - 1)
            self.covers[a] = (first // EIGHT, last // EIGHT)
        self.below = {
            a: [d for k, d in self.nodes if k < l
                and self.covers[a][0] <= self.covers[d][0] < self.covers[a][1]]
            for l, a in self.nodes
        }
        order = []
        for l, a in self.nodes:
            order += [(d, l) for d in self.below[a]] + [(a, 0)]
        self.blocks = len(self.mid) + len(order)
        self.high = {key: len(self.mid) + i for i, key in enumerate(order)}
        self.rhs = 3 + len(self.nodes)
        self.high_rhs = {a: 3 + i for i, (l, a) in enumerate(self.nodes)}


def kernel(
    chips, count, plan,
    rhs_h, inv_h, pan_h, mask_s, irhs_h, iinv_h, ipan_h,
    leaf_out, inner_out,
    v_rhs, v_inv, v_pan, i_hi, i_lo, p_hi, p_lo, leaf_t,
    terms, terms_in, pieces1, upd,
    gather, gsum, gchips, gout, tin,
    blocks, rblock, rhs_t, b_hi, b_lo,
    vin, win, wout, fwd, sol, solb, xhigh, full, leaf_acc, turned,
    in_sem, arr_sem, arr_rhs, put_send,
    ring_recv, ring_send, rring_recv, rring_send, sib_recv, sib_send, rsib_recv, rsib_send,
    fw_recv, fw_send, rfw_recv, rfw_send,
    t_recv, t_send, a1_recv, a1_send,
    g_recv, g_send, gz_recv, gz_send, tin_recv, tin_send,
    v_recv, v_send, w_recv, w_send, x_send, down_recv, down_send,
    ag_recv, ag_send, left_send, pair_recv, pair_send,
):
    top = pan_h.shape[0]
    width, nrhs = v_rhs.shape
    member = lax.axis_index("grp")
    j = lax.axis_index("row")
    z, c = lax.div(member, 2), lax.rem(member, 2)
    other = 1 - c
    parity = lax.rem(j, 2)
    place = lax.rem(j, EIGHT)
    group = lax.div(j, EIGHT)
    start = j - place
    host2 = start + 2
    odd, even = parity == 1, parity == 0
    is2 = place == 2
    is3 = j == plan.host3
    mate = jnp.where(odd, j - 1, j + 1)
    lev = jnp.int32(1)
    for bit in range(1, top):
        lev = lev + (lax.rem(j, 2**bit) == 0).astype(jnp.int32)
    is0, is6 = place == 0, place == 6
    helps = jnp.logical_or(is0, is6)
    near = jnp.logical_not(jnp.logical_or(is0, place == 4))
    low = jnp.where(is6, top - 1, jnp.where(is0, 2 * (top - 1), 0))
    size = jnp.where(odd, top, jnp.where(is0, top - 2, top - 1))
    size = jnp.where(place == 4, 0, size)
    rlow = jnp.where(is6, 1, jnp.where(is0, 2, 0))
    rsize = jnp.where(place == 4, 0, 1)
    nmid = len(plan.mid)

    def at(zz=None, cc=None, jj=None):
        zz = z if zz is None else zz
        cc = c if cc is None else cc
        return {"grp": zz * 2 + cc, "row": j if jj is None else jj}

    def turn(step):
        return lax.rem(z + step + chips, chips)

    def remote(src, dst, send, recv, where):
        return pltpu.make_async_remote_copy(
            src_ref=src, dst_ref=dst, send_sem=send, recv_sem=recv,
            device_id=where, device_id_type=pl.DeviceIdType.MESH,
        )

    def local(src, dst, sem):
        return pltpu.make_async_copy(src, dst, sem)

    def await_bytes(ref, sem):
        pltpu.make_async_copy(ref, ref, sem).wait()

    rhs_in = local(rhs_h, v_rhs, in_sem.at[top])
    inv_in = local(inv_h, v_inv, in_sem.at[top + 1])
    rhs_in.start()
    inv_in.start()

    def panel_in(step):
        return local(pan_h.at[step], v_pan.at[step], in_sem.at[step])

    panel_in(0).start()

    def keep(l, slot):
        src = iinv_h if l == 0 else ipan_h.at[l - 1]
        local(src, blocks.at[slot, z, c], arr_sem.at[slot]).start()

    @pl.when(odd)
    def _():
        for l in [0] + list(range(2, top + 1)):
            keep(l, max(l - 1, 0))

    for key in (2, 6):
        @pl.when(place == key)
        def _(key=key):
            for l in [0] + list(range(3, top + 1)):
                keep(l, plan.mid[key, l])

    @pl.when(near)
    def _():
        local(irhs_h, rblock.at[rlow, z, c], arr_rhs.at[rlow]).start()

    for step in range(1, top):
        panel_in(step).start()

    barrier = pltpu.get_barrier_semaphore()

    def greet(where):
        pl.semaphore_signal(barrier, inc=1, device_id=where, device_id_type=pl.DeviceIdType.MESH)

    greet(at(cc=other))
    for step in range(1, chips):
        greet(at(zz=turn(step)))
    for step in range(chips):
        greet(at(zz=turn(step), jj=mate))

    for step in range(1, EIGHT):
        greet(at(jj=start + lax.rem(place + step, EIGHT)))

    @pl.when(is2)
    def _():
        greet(at(jj=plan.host3))

    @pl.when(is3)
    def _():
        for g in range(plan.groups):
            greet(at(jj=g * EIGHT + 2))
        for l, a in plan.nodes:
            greet(at(jj=a))

    @pl.when(is0)
    def _():
        greet(at(jj=plan.host3))

    expected = 2 * chips + EIGHT - 1 + jnp.where(is2, 1, 0) + jnp.where(is0, 1, 0)
    expected = expected + jnp.where(is3, plan.groups + len(plan.nodes), 0)

    def puts(slots, rhs_slots, key, levels, target):
        for n, l in enumerate([0] + levels):
            src = iinv_h if l == 0 else ipan_h.at[l - 1]
            slot = slots[key, l]
            yield remote(
                src, blocks.at[slot, z, c], put_send.at[n], arr_sem.at[slot], at(jj=target)
            )
        slot = rhs_slots[key]
        yield remote(
            irhs_h, rblock.at[slot, z, c], put_send.at[top], arr_rhs.at[slot], at(jj=target)
        )

    def each_put(act):
        @pl.when(place == 4)
        def _():
            for copy in puts(plan.mid, plan.mid_rhs, 4, list(range(4, top + 1)), start):
                act(copy)
        for l, a in plan.nodes:
            @pl.when(j == a)
            def _(l=l, a=a):
                levels = list(range(l + 1, top + 1))
                for copy in puts(plan.high, plan.high_rhs, a, levels, plan.host3):
                    act(copy)

    right, left = chips // 2, chips - 1 - chips // 2

    def heading(way, b):
        return (1 if way == 0 else -1) * (1 - 2 * lax.rem(b, 2))

    def ring(kind, way, step, b):
        ref = kind[0].at[b, turn(-step * heading(way, b)), c]
        return remote(
            ref, ref, kind[2].at[b], kind[3].at[way, step, b], at(zz=turn(heading(way, b)))
        )

    def ring_arrived(kind, way, step, b):
        src = turn(-(step + 1) * heading(way, b))
        await_bytes(kind[0].at[b, src, c], kind[3].at[way, step, b])
        pass_on(kind, b, src)

    kinds = (
        (blocks, arr_sem, ring_send, ring_recv, sib_send, sib_recv, fw_send, fw_recv),
        (rblock, arr_rhs, rring_send, rring_recv, rsib_send, rsib_recv, rfw_send, rfw_recv),
    )
    ranges = ((low, low + size), (rlow, rlow + rsize))
    ranges3 = (
        (nmid, jnp.where(is3, plan.blocks, nmid)),
        (3, jnp.where(is3, plan.rhs, 3)),
    )

    def pass_on(kind, b, src):
        @pl.when(passes(kind, b))
        def _():
            ref = kind[0].at[b, src, c]
            remote(ref, ref, kind[6].at[b], kind[7].at[b], at(jj=host2)).start()

    def first_step(ranges):
        for kind, (first, last) in zip(kinds, ranges):
            @pl.loop(first, last)
            def _(b):
                await_bytes(kind[0].at[b, z, c], kind[1].at[b])
                if right:
                    ring(kind, 0, 0, b).start()
                if left:
                    ring(kind, 1, 0, b).start()
                pass_on(kind, b, z)

    final = max(right, left)

    def next_step(step, ranges):
        for kind, (first, last) in zip(kinds, ranges):
            @pl.loop(first, last)
            def _(b):
                if step <= right:
                    ring_arrived(kind, 0, step - 1, b)
                    if step < right:
                        ring(kind, 0, step, b).start()
                if step <= left:
                    ring_arrived(kind, 1, step - 1, b)
                    if step < left:
                        ring(kind, 1, step, b).start()
                if step == final:
                    @pl.when(jnp.logical_not(passes(kind, b)))
                    def _():
                        share(kind, b).start()

    def passes(kind, b):
        return jnp.logical_and(helps, b < (nmid if kind[0] is blocks else 3))

    def share(kind, b):
        ref = kind[0].at[b, :, c]
        return remote(ref, ref, kind[4].at[b], kind[5].at[b], at(cc=other))

    def helped(kind, first, last):
        @pl.loop(first, last)
        def _(b):
            await_bytes(kind[0].at[b, :, c], kind[7].at[b])
            share(kind, b).start()

    def take_rhs(b):
        await_bytes(rblock.at[b, :, other], rsib_recv.at[b])
        rhs_t[b] = rblock[b].reshape(width, nrhs).T.reshape(rhs_t.shape[1:])

    def take_block(b):
        await_bytes(blocks.at[b, :, other], sib_recv.at[b])
        hi, lo = split(blocks[b].reshape(width, width))
        b_hi[b] = hi
        b_lo[b] = lo

    def block(b):
        return b_hi[b], b_lo[b]

    rhs_in.wait()
    inv_in.wait()
    hi, lo = split(v_inv[...])
    i_hi[...] = hi
    i_lo[...] = lo
    forward = product((hi, lo), split(v_rhs[...])).T
    leaf_t[...] = forward
    forward = split(forward)

    def swap_cores(l):
        return remote(
            terms.at[other, :, l], terms_in.at[:, l], t_send, t_recv.at[l], at(cc=other)
        )

    @pl.loop(0, top)
    def _(l):
        panel_in(l).wait()
        hi, lo = split(v_pan[l])
        p_hi[l] = hi
        p_lo[l] = lo
        term = product(forward, (hi, lo)) * mask_s[l].astype(F32)
        terms[:, :, l] = term.reshape(2, chips, -1, width)

    pl.semaphore_wait(barrier, expected)

    for l in range(top):
        swap_cores(l).start()
    each_put(lambda copy: copy.start())
    nowhere = lambda pair: (pair[0], jnp.where(near, pair[1], pair[0]))
    first_step([nowhere(pair) for pair in ranges])

    def add_cores(l):
        await_bytes(terms_in.at[:, l], t_recv.at[l])
        terms[c, :, l] = terms[c, :, l] + terms_in[:, l]

    def send_first(step):
        return remote(
            terms.at[c, turn(step), 0], pieces1.at[parity, z],
            a1_send.at[0 if step else 1], a1_recv.at[parity], at(zz=turn(step), jj=jnp.where(odd, j, mate)),
        )

    add_cores(0)

    @pl.when(even)
    def _():
        send_first(0).start()

    for step in range(1, chips):
        send_first(step).start()

    def collect(i):
        at_place, l, first, n = plan.items[i]
        return remote(
            terms.at[c, :, l - 1], gather.at[place], g_send.at[i], g_recv, at(jj=start + at_place)
        )

    def each_collect(l, act):
        for i, (at_place, level, first, n) in enumerate(plan.items):
            if level == l:
                @pl.when(jnp.logical_and(
                    place != at_place, jnp.logical_and(place >= first, place < first + n)
                ))
                def _(i=i):
                    act(collect(i))

    for l in range(2, top + 1):
        add_cores(l - 1)
        each_collect(l, lambda copy: copy.start())

    holds, my_item, my_level = place < 0, jnp.int32(0), jnp.int32(0)
    for i, (at_place, l, first, n) in enumerate(plan.items):
        mine = place == at_place
        holds = jnp.logical_or(holds, mine)
        my_item = jnp.where(mine, i, my_item)
        my_level = jnp.where(mine, l - 1, my_level)
    sources = jnp.where(my_item < 2, 4, EIGHT)
    origin = jnp.where(my_item == 1, 4, 0)

    def to_chip(step):
        return remote(gsum.at[turn(step)], gchips.at[z], gz_send, gz_recv, at(zz=turn(step)))

    def to_host():
        return remote(gout, tin.at[my_item], tin_send, tin_recv.at[my_item], at(jj=host2))

    def sum_places():
        @pl.when(holds)
        def _():
            @pl.when(my_item < 2)
            def _():
                await_bytes(gather.at[0:3], g_recv)

            @pl.when(my_item >= 2)
            def _():
                await_bytes(gather.at[0 : EIGHT - 1], g_recv)

            gsum[...] = terms[c, :, my_level]

            @pl.loop(1, sources)
            def _(k):
                r = origin + lax.rem(place - origin + k, sources)
                gsum[...] = gsum[...] + gather[r]

            for step in range(1, chips):
                to_chip(step).start()

    def sum_chips():
        @pl.when(holds)
        def _():
            await_bytes(gchips.at[0 : chips - 1], gz_recv)
            total = gsum[z]
            for step in range(1, chips):
                total = total + gchips[turn(step)]
            gout[...] = total
            to_host().start()

    far = lambda pair: (pair[0], jnp.where(near, pair[0], pair[1]))
    first_step([far(pair) for pair in ranges])
    first_step(ranges3)
    between = (final + 1) // 2
    for step in range(1, final + 1):
        next_step(step, ranges)
        next_step(step, ranges3)
        if step == between:
            sum_places()
    sum_chips()

    def send_v(l):
        return remote(
            upd.at[l - 2], vin.at[l - 2, lax.div(place, 2)], v_send.at[l - 2], v_recv.at[l - 2],
            at(jj=host2),
        )

    @pl.when(odd)
    def _():
        take_rhs(0)
        take_block(0)
        await_bytes(pieces1.at[0], a1_recv.at[0])
        await_bytes(pieces1.at[0, 0 : chips - 1], a1_recv.at[1])
        total = terms[c, z, 0] + pieces1[0, z]
        for step in range(1, chips):
            total = total + (pieces1[0, turn(step)] + pieces1[1, turn(step)])
        fwd[0] = thin(rhs_t[0, c, z] - total, block(0), NT)
        @pl.loop(2, top + 1)
        def _(l):
            take_block(l - 1)
            upd[l - 2] = thin(fwd[0], block(l - 1), NN)
            send_v(l).start()

    mid = plan.mid
    order = (1, 3, 5, 7, 0, 4, 6)

    def send_w(l):
        return remote(
            wout.at[l - 4], win.at[l - 4, group], w_send.at[l - 4], w_recv.at[l - 4],
            at(jj=plan.host3),
        )

    def arrived(l):
        await_bytes(vin.at[l - 2], v_recv.at[l - 2])
        for i, item in enumerate(plan.items):
            if item[1] == l:
                await_bytes(tin.at[i], tin_recv.at[i])

    def slots(l, first, last):
        total = tin[l - 1 if l > 2 else first // 2]
        for r in range(first, last):
            total = total + vin[l - 2, r]
        return total

    @pl.when(is2)
    def _():
        helped(kinds[1], 1, 3)
        helped(kinds[0], top - 1, nmid)
        for b in range(3):
            take_rhs(b)
        pl.loop(0, nmid)(take_block)
        arrived(2)
        fwd[0] = thin(rhs_t[0, c, z] - slots(2, 0, 2), block(mid[2, 0]), NT)
        fwd[1] = thin(rhs_t[1, c, z] - slots(2, 2, 4), block(mid[6, 0]), NT)
        arrived(3)
        fwd[2] = thin(
            rhs_t[2, c, z] - slots(3, 0, 4) - thin(fwd[0], block(mid[2, 3]), NN)
            - thin(fwd[1], block(mid[6, 3]), NN),
            block(mid[4, 0]), NT,
        )
        for l in range(4, top + 1):
            arrived(l)
            wout[l - 4] = slots(l, 0, 4) + (
                thin(fwd[0], block(mid[2, l]), NN) + thin(fwd[1], block(mid[6, l]), NN)
            ) + thin(fwd[2], block(mid[4, l]), NN)
            send_w(l).start()

    level_of = {a: l for l, a in plan.nodes}

    def send_x(a, g):
        n = plan.high_rhs[a] - 3
        l = level_of[a]
        return remote(
            xhigh.at[n], sol.at[l - 1], x_send.at[n, g], down_recv.at[l - 1],
            at(jj=g * EIGHT + 2),
        )

    @pl.when(is3)
    def _():
        for b in range(3, plan.rhs):
            take_rhs(b)
        pl.loop(nmid, plan.blocks)(take_block)
        for n, (l, a) in enumerate(plan.nodes):
            if n == 0 or plan.nodes[n - 1][0] != l:
                await_bytes(win.at[l - 4], w_recv.at[l - 4])
            total = rhs_t[3 + n, c, z]
            for g in range(*plan.covers[a]):
                total = total - win[l - 4, g]
            for d in plan.below[a]:
                total = total - thin(fwd[plan.high_rhs[d] - 3], block(plan.high[d, l]), NN)
            fwd[n] = thin(total, block(plan.high[a, 0]), NT)
        for l, a in reversed(plan.nodes):
            n = plan.high_rhs[a] - 3
            rest = fwd[n]
            for k, up in plan.nodes:
                if a in plan.below[up]:
                    rest = rest - thin(xhigh[plan.high_rhs[up] - 3], block(plan.high[a, k]), NT)
            xhigh[n] = thin(rest, block(plan.high[a, 0]), NN)
            for g in range(*plan.covers[a]):
                send_x(a, g).start()

    leaf_acc[...] = jnp.zeros_like(leaf_acc)

    def send_down(l, r, src=None):
        src = sol.at[l - 1] if src is None else src
        return remote(
            src, sol.at[l - 1], down_send.at[l - 1], down_recv.at[l - 1], at(jj=start + r)
        )

    def spread(l):
        full[l - 1, c, z] = sol[l - 1]
        for step in range(1, chips):
            remote(
                sol.at[l - 1], full.at[l - 1, c, z], ag_send.at[l - 1], ag_recv.at[l - 1],
                at(zz=turn(step)),
            ).start()

    def spread_left(step):
        return remote(
            sol.at[0], full.at[0, c, z], left_send, ag_recv.at[0], at(zz=turn(step), jj=mate)
        )

    @pl.when(is2)
    def _():
        rest = [fwd[0], fwd[1], fwd[2]]
        for l in range(top, 3, -1):
            await_bytes(sol.at[l - 1], down_recv.at[l - 1])
            for r in order:
                send_down(l, r).start()
            for n, key in enumerate((2, 6, 4)):
                rest[n] = rest[n] - thin(sol[l - 1], block(mid[key, l]), NT)
            if l > 4:
                spread(l)
        sol[2] = thin(rest[2], block(mid[4, 0]), NN)
        for r in order:
            send_down(3, r).start()
        for n, key in enumerate((2, 6)):
            rest[n] = rest[n] - thin(sol[2], block(mid[key, 3]), NT)
        sol[1] = thin(rest[0], block(mid[2, 0]), NN)
        solb[...] = thin(rest[1], block(mid[6, 0]), NN)
        for r in order:
            send_down(2, r, None if r < 4 else solb).start()
        for l in range(min(top, 4), 1, -1):
            spread(l)

    @pl.when(odd)
    def _():
        rest = fwd[0]
        for l in range(top, 1, -1):
            await_bytes(sol.at[l - 1], down_recv.at[l - 1])
            rest = rest - thin(sol[l - 1], block(l - 1), NT)
            if l > 3:
                spread(l)
        sol[0] = thin(rest, block(0), NN)
        spread(1)
        for step in range(chips):
            spread_left(step).start()
        for l in (3, 2):
            spread(l)

    @pl.when(jnp.logical_and(even, jnp.logical_not(is2)))
    def _():
        for l in range(top, 1, -1):
            await_bytes(sol.at[l - 1], down_recv.at[l - 1])
            spread(l)

    def pair(l):
        return remote(full.at[l, c], full.at[l, c], pair_send.at[l], pair_recv.at[l], at(cc=other))

    def leaf_back(l):
        await_bytes(full.at[l, other], pair_recv.at[l])
        ancestor = split(full[l].reshape(nrhs, width))
        leaf_acc[...] = leaf_acc[...] + mask_s[l].astype(F32) * product(
            ancestor, (p_hi[l], p_lo[l]), NT
        )

    @pl.loop(0, top)
    def _(i):
        l = top - 1 - i

        @pl.when(jnp.logical_and(l == 0, even))
        def _():
            await_bytes(full.at[0, c], ag_recv.at[0])

        @pl.when(jnp.logical_or(l > 0, odd))
        def _():
            await_bytes(full.at[l, c, 0 : chips - 1], ag_recv.at[l])

        pair(l).start()

        @pl.when(i >= 1)
        def _():
            leaf_back(l + 1)

    def own_rows():
        share_rows = inner_out.shape[0]
        turned[...] = full[lev - 1].reshape(nrhs, width).T
        rows = pl.ds(pl.multiple_of(member * share_rows, share_rows), share_rows)
        inner_out[...] = turned[rows, :]

    pl.when(even)(own_rows)
    leaf_back(0)
    rest = split(leaf_t[...] - leaf_acc[...])
    leaf_out[...] = product(rest, (i_hi[...], i_lo[...])).T
    pl.when(odd)(own_rows)

    each_put(lambda copy: copy.wait_send())
    for some in (ranges, ranges3):
        for kind, (first, last) in zip(kinds, some):
            @pl.loop(first, last)
            def _(b):
                await_bytes(kind[0].at[b, 0 : chips - 1, 0], kind[2].at[b])
                gone = jnp.where(passes(kind, b), 1, 0)

                @pl.when(gone == 1)
                def _():
                    await_bytes(kind[0].at[b, :, c], kind[6].at[b])

                @pl.when(gone == 0)
                def _():
                    await_bytes(kind[0].at[b, :, c], kind[4].at[b])

    @pl.when(is2)
    def _():
        for kind, (first, last) in zip(kinds, ((top - 1, nmid), (1, 3))):
            @pl.loop(first, last)
            def _(b):
                await_bytes(kind[0].at[b, :, c], kind[4].at[b])
    await_bytes(terms.at[0], t_send)
    await_bytes(pieces1.at[0, 0 : chips - 1], a1_send.at[0])
    for l in range(2, top + 1):
        each_collect(l, lambda copy: copy.wait_send())

    @pl.when(holds)
    def _():
        await_bytes(gchips.at[0 : chips - 1], gz_send)
        to_host().wait_send()

    @pl.when(odd)
    def _():
        for l in range(2, top + 1):
            send_v(l).wait_send()

    @pl.when(is2)
    def _():
        for l in range(4, top + 1):
            send_w(l).wait_send()
        for l in range(2, top + 1):
            await_bytes(gather.at[0 : EIGHT - 1, 0], down_send.at[l - 1])

    @pl.when(is3)
    def _():
        for l, a in plan.nodes:
            for g in range(*plan.covers[a]):
                send_x(a, g).wait_send()

    @pl.loop(1, top)
    def _(l):
        await_bytes(full.at[l, 0, 0 : chips - 1], ag_send.at[l])

    @pl.when(odd)
    def _():
        await_bytes(full.at[0, 0, 0 : chips - 1], ag_send.at[0])
        await_bytes(full.at[0, 0], left_send)

    @pl.when(even)
    def _():
        send_first(0).wait_send()

    @pl.loop(0, top)
    def _(l):
        pair(l).wait_send()


def per_device(leaf_rhs, leaf_inv, leaf_panel, leaf_mask, inner_rhs, inner_inv, inner_panel):
    members, count = lax.axis_size("grp"), lax.axis_size("row")
    chips = members // 2
    width, nrhs = leaf_rhs.shape[2:]
    top = leaf_panel.shape[2]
    share, cols = width // members, nrhs // members
    plan = Plan(top, count)
    nb, nr, high = plan.blocks, plan.rhs, top - 3
    hbm = pl.BlockSpec(memory_space=pl.ANY)
    dma = pltpu.SemaphoreType.DMA
    steps = max(chips // 2, 1)
    v = pltpu.VMEM
    call = pl.pallas_call(
        functools.partial(kernel, chips, count, plan),
        out_shape=(
            pltpu.VMEM((width, nrhs), F32),
            pltpu.VMEM((share, nrhs), F32),
        ),
        in_specs=[hbm, hbm, hbm, pl.BlockSpec(memory_space=pltpu.SMEM), hbm, hbm, hbm],
        out_specs=[pl.BlockSpec(memory_space=pltpu.VMEM)] * 2,
        scratch_shapes=[
            v((width, nrhs), F32),
            v((width, width), F32),
            v((top, width, width), F32),
            v((width, width), BF16),
            v((width, width), BF16),
            v((top, width, width), BF16),
            v((top, width, width), BF16),
            v((nrhs, width), F32),
            v((2, chips, top, cols, width), F32),
            v((chips, top, cols, width), F32),
            v((2, chips, cols, width), F32),
            v((top - 1, cols, width), F32),
            v((EIGHT, chips, cols, width), F32),
            v((chips, cols, width), F32),
            v((chips, cols, width), F32),
            v((cols, width), F32),
            v((top, cols, width), F32),
            v((nb, chips, 2, share, width), F32),
            v((nr, chips, 2, share, nrhs), F32),
            v((nr, 2, chips, cols, width), F32),
            v((nb, width, width), BF16),
            v((nb, width, width), BF16),
            v((top - 1, 4, cols, width), F32),
            v((high, plan.groups, cols, width), F32),
            v((high, cols, width), F32),
            v((max(3, len(plan.nodes)), cols, width), F32),
            v((top, cols, width), F32),
            v((cols, width), F32),
            v((len(plan.nodes), cols, width), F32),
            v((top, 2, chips, cols, width), F32),
            v((nrhs, width), F32),
            v((width, nrhs), F32),
            dma((top + 2,)),
            dma((nb,)),
            dma((nr,)),
            dma((top + 1,)),
            dma((2, steps, nb)),
            dma((nb,)),
            dma((2, steps, nr)),
            dma((nr,)),
            dma((nb,)),
            dma((nb,)),
            dma((nr,)),
            dma((nr,)),
            dma((nb,)),
            dma((nb,)),
            dma((3,)),
            dma((3,)),
            dma((top,)),
            dma,
            dma((2,)),
            dma((2,)),
            dma,
            dma((top,)),
            dma,
            dma,
            dma((top,)),
            dma,
            dma((top - 1,)),
            dma((top - 1,)),
            dma((high,)),
            dma((high,)),
            dma((len(plan.nodes), plan.groups)),
            dma((top,)),
            dma((top,)),
            dma((top,)),
            dma((top,)),
            dma,
            dma((top,)),
            dma((top,)),
        ],
        compiler_params=pltpu.CompilerParams(
            collective_id=0, has_side_effects=True, vmem_limit_bytes=60 * 2**20
        ),
    )
    leaf, inner = call(
        leaf_rhs[0, 0], leaf_inv[0, 0], leaf_panel[0, 0], leaf_mask[0, 0],
        inner_rhs[0], inner_inv[0], inner_panel[0],
    )
    return leaf[None, None], inner[None]


def solution(mesh):
    in_specs = (
        P("row", "grp", None, None),
        P("row", "grp", None, None),
        P("row", "grp", None, None, None),
        P("row", "grp", None),
        P("row", "grp", None),
        P("row", "grp", None),
        P("row", None, "grp", None),
    )
    out_specs = (P("row", "grp", None, None), P("row", "grp", None))
    return jax.shard_map(
        per_device, mesh=mesh, in_specs=in_specs, out_specs=out_specs, check_vma=False
    )
```
